128 devices in a mesh: seq: 16 (over y_hi, z, core), enc: 8 (over x, y_lo).
Axes of the slice: x: 4, y: 4 (y_hi: 2, y_lo: 2; y = y_hi * 2 + y_lo), z: 4, core: 2. Of those that a mesh axis runs over, the one named last changes fastest.
Arguments:
- queries: bfloat16 [24576, 2048], P(('seq', 'enc')), may hold values from -10.2 to 10.2
- cond: bfloat16 [24576, 1024], P(('seq', 'enc')), may hold values from -10.2 to 10.2
- database: bfloat16 [256, 128, 1024], P('enc'), may hold values from -6 to 6
- neighbour_ids: int32 [384, 2], P(('seq', 'enc')), may hold values from 0 to 31
- owner_map: int32 [384, 2], P(('seq', 'enc')), may hold values from 0 to 7, as said below
- norm_gain: float32 [1024], replicated, may hold values from 0.1 to 1.9
- w_query_enc: bfloat16 [1024, 512], replicated, may hold values from -0.1875 to 0.1875
- w_out_enc: bfloat16 [512, 1024], replicated, may hold values from -0.25 to 0.25
- w_key_dec: bfloat16 [1024, 2048], replicated, may hold values from -0.1875 to 0.1875
- w_value_dec: bfloat16 [1024, 2048], replicated, may hold values from -0.1875 to 0.1875
- cotangent: bfloat16 [24576, 2048], P(('seq', 'enc')), may hold values from -6 to 6
Outputs:
- attended: bfloat16 [24576, 2048], P(('seq', 'enc'))
- grad_queries: bfloat16 [24576, 2048], P(('seq', 'enc'))
- grad_cond: bfloat16 [24576, 1024], P(('seq', 'enc'))
- grad_query_enc: float32 [1024, 512], P(('seq', 'enc'))
- grad_out_enc: float32 [512, 1024], P(('seq', 'enc'))
- grad_key_dec: float32 [1024, 2048], P(('seq', 'enc'))
- grad_value_dec: float32 [1024, 2048], P(('seq', 'enc'))
The draws below stay inside these ranges and needn't reach their ends.
Inputs may be any that keep to these rules, and one draw needn't show every extreme that they name: `owner_map`: of the 6 neighbours of one device's spans at most 1 have the same owner; in every group of 8 devices along enc one owner gets exactly 1 from every device of the group.
All inputs are finite; a program needn't handle non-finite values.
Results may differ from the reference program's by a relative error of at most 0.018.
Values may be sent and summed in bfloat16 or wider, within the bound.
A program may use at most 192 MiB of HBM per device.

```python
import jax
import jax.numpy as jnp
from jax import lax

DE = 1024
HEADS_D = 16
HEADS_E = 8
SPAN = 64
NEIGH = 2
NLEN = 128
DB_DEV = 32
HD_D = 2048
HD_E = 512
UNITS = 6
OWNERS = 8
CAP = 1
TOKENS = 24576
SPANS = 384
DB_ROWS = 256


def draw_queries(key, part):
    key = jax.random.fold_in(key, 3)
    first = jax.random.fold_in(key, 0)
    base = jnp.clip(jax.random.normal(first, (TOKENS, HD_D), jnp.float32), -6.0, 6.0)
    return base.astype(jnp.bfloat16)


def draw_cond(key, part):
    key = jax.random.fold_in(key, 5)
    first = jax.random.fold_in(key, 0)
    base = jnp.clip(jax.random.normal(first, (TOKENS, 2 * HD_E), jnp.float32), -6.0, 6.0)
    return base.astype(jnp.bfloat16)


def draw_owner_map(key, part):
    key = jax.random.fold_in(key, 7)
    devices = SPANS * NEIGH // UNITS
    groups = devices // OWNERS
    first, second, third = jax.random.split(key, 3)
    full_owner = jax.random.randint(first, (groups,), 0, OWNERS)
    full_device = jnp.repeat(full_owner, OWNERS)
    others = OWNERS * CAP - CAP
    shuffled = jax.vmap(lambda one: jax.random.permutation(one, others))(jax.random.split(second, devices))
    chosen = shuffled[:, :UNITS - CAP]
    lowest = full_device[:, None] * CAP
    rest = jnp.where(chosen >= lowest, chosen + CAP, chosen)
    full = lowest + jnp.arange(CAP)[None, :]
    every = jnp.concatenate([full, rest], axis=1)
    order = jax.vmap(lambda one: jax.random.permutation(one, UNITS))(jax.random.split(third, devices))
    placed = jnp.take_along_axis(every, order, axis=1)
    return (placed // CAP).astype(jnp.int32).reshape(SPANS, NEIGH)


def touch_ends(drawn, own_key, least, top_value):
    longest = drawn.shape.index(max(drawn.shape))
    spots = []
    for shift in (0, 1):
        where = [jax.random.randint(jax.random.fold_in(own_key, axis), (), 0, length) for axis, length in enumerate(drawn.shape)]
        where[longest] = (where[longest] + shift) % drawn.shape[longest]
        spots.append(tuple(where))
    return drawn.at[spots[0]].set(least).at[spots[1]].set(top_value)


def shard_levels(key, dims, pieces, low, top_value):
    loudness = 1.0
    for position, shards_of in pieces:
        steps = jax.random.uniform(jax.random.fold_in(jax.random.fold_in(key, 6), position), (shards_of,), jnp.float32, low / len(pieces), top_value / len(pieces))
        loudness = loudness * jnp.repeat(jnp.exp(steps), dims[position] // shards_of).reshape((-1,) + (1,) * (len(dims) - 1 - position))
    return loudness


def gaussian(stream_key, extent, width, bound, shards=(), kind=jnp.bfloat16):
    array = width * jax.random.normal(stream_key, extent, jnp.float32)
    if shards:
        array = array * shard_levels(stream_key, extent, shards, -0.22, 0.18)
    return jnp.clip(array, -bound, bound).astype(kind)


def setup_inputs(seed: int = 0) -> dict:
    arg_keys = jax.random.split(jax.random.key(seed), 12)
    queries = draw_queries(jax.random.fold_in(arg_keys[11], 71), 0)
    cond = draw_cond(jax.random.fold_in(arg_keys[11], 71), 0)
    database = gaussian(arg_keys[2], (DB_ROWS, NLEN, DE), 1.0, 6.0, ((0, 8),))
    neighbour_ids = touch_ends(jax.random.randint(arg_keys[3], (SPANS, NEIGH), 0, DB_DEV), jax.random.fold_in(arg_keys[3], 1), 0, DB_DEV - 1).astype(jnp.int32)
    owner_map = draw_owner_map(jax.random.fold_in(arg_keys[11], 71), 0)
    norm_gain = jnp.clip(1.0 + 0.18 * jax.random.normal(arg_keys[5], (DE,), jnp.float32), 0.1, 1.9)
    w_query_enc = gaussian(arg_keys[6], (DE, HD_E), DE ** -0.5, 0.1875)
    w_out_enc = gaussian(arg_keys[7], (HD_E, DE), HD_E ** -0.5, 0.25)
    w_key_dec = gaussian(arg_keys[8], (DE, HD_D), DE ** -0.5, 0.1875)
    w_value_dec = gaussian(arg_keys[9], (DE, HD_D), DE ** -0.5, 0.1875)
    cotangent = gaussian(arg_keys[10], (TOKENS, HD_D), 1.0, 6.0, ((0, 128),))
    return dict(queries=queries, cond=cond, database=database, neighbour_ids=neighbour_ids, owner_map=owner_map, norm_gain=norm_gain, w_query_enc=w_query_enc, w_out_enc=w_out_enc, w_key_dec=w_key_dec, w_value_dec=w_value_dec, cotangent=cotangent)


EPS = 1e-06

def rounded(value):
    return lax.optimization_barrier(value.astype(jnp.bfloat16))

def attend(query, keys, values, heads):
    size = query.shape[-1] // heads
    scale = size ** (-0.5)
    q_four = query.reshape(query.shape[:-1] + (heads, size)).astype(jnp.float32)
    k_four = keys.reshape(keys.shape[:-1] + (heads, size)).astype(jnp.float32)
    v_four = values.reshape(values.shape[:-1] + (heads, size)).astype(jnp.float32)
    scores = jnp.einsum('bqhd,bkhd->bhqk', q_four, k_four) * scale
    probs = jax.nn.softmax(scores, axis=-1)
    weights = rounded(probs).astype(jnp.float32)
    mixed = jnp.einsum('bhqk,bkhd->bqhd', weights, v_four)
    return (mixed.reshape(query.shape), probs)

def attend_back(grad_out, query, keys, values, probs, heads):
    size = query.shape[-1] // heads
    scale = size ** (-0.5)
    g_four = grad_out.reshape(grad_out.shape[:-1] + (heads, size)).astype(jnp.float32)
    q_four = query.reshape(query.shape[:-1] + (heads, size)).astype(jnp.float32)
    k_four = keys.reshape(keys.shape[:-1] + (heads, size)).astype(jnp.float32)
    v_four = values.reshape(values.shape[:-1] + (heads, size)).astype(jnp.float32)
    weights = rounded(probs).astype(jnp.float32)
    d_weights = jnp.einsum('bqhd,bkhd->bhqk', g_four, v_four)
    d_values = jnp.einsum('bhqk,bqhd->bkhd', weights, g_four)
    d_scores = probs * (d_weights - lax.optimization_barrier(jnp.sum(d_weights * probs, axis=-1, keepdims=True))) * scale
    d_scores = rounded(d_scores).astype(jnp.float32)
    d_query = jnp.einsum('bhqk,bkhd->bqhd', d_scores, k_four)
    d_keys = jnp.einsum('bhqk,bqhd->bkhd', d_scores, q_four)
    return (d_query.reshape(query.shape), d_keys.reshape(keys.shape), d_values.reshape(values.shape))

def outer_sum(left, right):
    left_flat = left.reshape(-1, left.shape[-1])
    right_flat = right.reshape(-1, right.shape[-1])
    return jnp.dot(left_flat.T, right_flat, preferred_element_type=jnp.float32)

def back_project(grad, weight):
    return jnp.dot(grad, weight.T, preferred_element_type=jnp.float32)

def encode(rows, keys, values, gain, w_query, w_out):
    wide = rows.astype(jnp.float32)
    inverse = lax.rsqrt(lax.optimization_barrier(jnp.mean(wide * wide, axis=-1, keepdims=True)) + EPS)
    normed = rounded(wide * inverse * gain)
    query = rounded(jnp.dot(normed, w_query, preferred_element_type=jnp.float32))
    mixed, probs = attend(query, keys, values, HEADS_E)
    mixed = rounded(mixed)
    encoded = rounded(wide + jnp.dot(mixed, w_out, preferred_element_type=jnp.float32))
    return (encoded, (normed, query, probs, mixed))

def encode_back(grad, keys, values, saved, w_query, w_out):
    normed, query, probs, mixed = saved
    g_out = outer_sum(mixed, grad)
    d_mixed = rounded(back_project(grad, w_out))
    d_query, d_keys, d_values = attend_back(d_mixed, query, keys, values, probs, HEADS_E)
    g_query = outer_sum(normed, rounded(d_query))
    unit_grad = jnp.concatenate([rounded(d_keys), rounded(d_values)], axis=-1)
    return (g_query, g_out, unit_grad)

def cross_step(span_queries, span_grads, sources, w_key, w_value):
    dec_keys = rounded(jnp.dot(sources, w_key, preferred_element_type=jnp.float32))
    dec_values = rounded(jnp.dot(sources, w_value, preferred_element_type=jnp.float32))
    mixed, probs = attend(span_queries, dec_keys, dec_values, HEADS_D)
    d_query, d_keys, d_values = attend_back(span_grads, span_queries, dec_keys, dec_values, probs, HEADS_D)
    dk_round = rounded(d_keys)
    dv_round = rounded(d_values)
    grad_sources = rounded(back_project(dk_round, w_key) + back_project(dv_round, w_value))
    return (rounded(mixed), rounded(d_query), grad_sources, outer_sum(sources, dk_round), outer_sum(sources, dv_round))

def reference(queries, cond, database, neighbour_ids, owner_map, norm_gain, w_query_enc, w_out_enc, w_key_dec, w_value_dec, cotangent):
    width_e = w_query_enc.shape[1]
    table_rows = (owner_map * DB_DEV + neighbour_ids).astype(jnp.int32)

    def step(carry, index):
        acc_query, acc_out, acc_key, acc_value = carry
        before = jnp.maximum(index - 1, 0).astype(jnp.int32)
        valid = index > 0
        picked = lax.dynamic_index_in_dim(table_rows, before, 0, keepdims=False)
        rows = jnp.take(database, picked, axis=0)
        cond_rows = lax.dynamic_slice_in_dim(cond, before * SPAN, SPAN, 0)
        keys = jnp.broadcast_to(cond_rows[None, :, :width_e], (NEIGH, SPAN, width_e))
        values = jnp.broadcast_to(cond_rows[None, :, width_e:], (NEIGH, SPAN, width_e))
        encoded, saved = encode(rows, keys, values, norm_gain, w_query_enc, w_out_enc)
        encoded = jnp.where(valid, encoded, jnp.zeros_like(encoded))
        span_queries = lax.dynamic_slice_in_dim(queries, index * SPAN, SPAN, 0)[None]
        span_grads = lax.dynamic_slice_in_dim(cotangent, index * SPAN, SPAN, 0)[None]
        sources = encoded.reshape(1, NEIGH * NLEN, encoded.shape[-1])
        mixed, d_query, grad_sources, g_key, g_value = cross_step(span_queries, span_grads, sources, w_key_dec, w_value_dec)
        grad_encoded = grad_sources.reshape(NEIGH, NLEN, encoded.shape[-1])
        grad_encoded = jnp.where(valid, grad_encoded, jnp.zeros_like(grad_encoded))
        g_query, g_out, unit_grad = encode_back(grad_encoded, keys, values, saved, w_query_enc, w_out_enc)
        cond_grad = lax.optimization_barrier(jnp.sum(unit_grad.astype(jnp.float32), axis=0)).astype(jnp.bfloat16)
        carry = (acc_query + g_query, acc_out + g_out, acc_key + g_key, acc_value + g_value)
        return (carry, (mixed[0], d_query[0], cond_grad))
    start = (jnp.zeros(w_query_enc.shape, jnp.float32), jnp.zeros(w_out_enc.shape, jnp.float32), jnp.zeros(w_key_dec.shape, jnp.float32), jnp.zeros(w_value_dec.shape, jnp.float32))
    totals, (mixed_all, dq_all, cond_all) = lax.scan(step, start, jnp.arange(SPANS, dtype=jnp.int32))
    attended = mixed_all.reshape(TOKENS, HD_D)
    grad_queries = dq_all.reshape(TOKENS, HD_D)
    tail = jnp.zeros((1, SPAN, 2 * width_e), jnp.bfloat16)
    grad_cond = jnp.concatenate([cond_all[1:], tail], axis=0).reshape(TOKENS, 2 * width_e)
    return (attended, grad_queries, grad_cond, totals[0], totals[1], totals[2], totals[3])
```

```python
import functools

import jax
import jax.numpy as jnp
from jax import lax
from jax.experimental import pallas as pl
from jax.experimental.pallas import tpu as pltpu
from jax.sharding import PartitionSpec as P

HEADS_D = 16
HEADS_E = 8
SPAN = 64
NEIGH = 2
NLEN = 128
EPS = 1e-06
MESH = pl.DeviceIdType.MESH

ORDERS = (
    (("x", 0), ("x", 1), ("y", 0), ("y", 1), ("z", 0), ("z", 1)),
    (("y", 0), ("y", 1), ("z", 0), ("z", 1), ("x", 0), ("x", 1)),
    (("z", 0), ("z", 1), ("x", 0), ("x", 1), ("y", 0), ("y", 1)),
    (("x", 1), ("x", 0), ("z", 1), ("z", 0), ("y", 1), ("y", 0)),
    (("y", 1), ("y", 0), ("x", 1), ("x", 0), ("z", 1), ("z", 0)),
)
BASES = (0, 64, 96, 112, 120, 124, 126)
WIDTH = 512


def gray(v):
    return (((v + 1) // 2) % 2, v // 2)


def ungray(bits):
    return bits[1] * 2 + (bits[0] + bits[1]) % 2


def place():
    s, e = lax.axis_index("seq"), lax.axis_index("enc")
    return dict(core=s % 2, z=(s // 2) % 4, y=(s // 8) * 2 + e % 2, x=e // 2)


def device_of(at):
    y = at["y"]
    return ((y // 2) * 8 + at["z"] * 2 + at["core"], at["x"] * 2 + y % 2)


def flipped(at, axis, bit):
    there = dict(at)
    if axis == "core":
        there["core"] = 1 - at["core"]
    else:
        bits = list(gray(at[axis]))
        bits[bit] = 1 - bits[bit]
        there[axis] = ungray(bits)
    return there


def chunk_row(order, c, core):
    bits = {"x": [0, 0], "y": [0, 0], "z": [0, 0]}
    for place_of, (axis, bit) in enumerate(order):
        bits[axis][bit] = (c // (32 >> place_of)) % 2
    return sum(
        part * scale
        for part, scale in zip(
            (bits["y"][1], ungray(bits["z"]), core, ungray(bits["x"]), (bits["y"][0] + bits["y"][1]) % 2),
            (64, 16, 8, 2, 1),
        )
    )


def reduce_kernel(gk, gv, gq, go, out, sbuf, rbuf, acc, ssem, rsem):
    at = place()
    partners = [flipped(at, "core", 0)] + [flipped(at, a, b) for a in "xyz" for b in (0, 1)]
    barrier = pltpu.get_barrier_semaphore()
    for there in partners:
        pl.semaphore_signal(barrier, inc=1, device_id=device_of(there), device_id_type=MESH)
    pl.semaphore_wait(barrier, len(partners))

    def load(k, p):
        if k < 4:
            cols = pl.ds(k * WIDTH, WIDTH)
            return jnp.concatenate([gk[p, :, cols], gv[p, :, cols]], axis=0)
        return jnp.concatenate([gq[p], go[p]], axis=0)

    def copy(k, j):
        half = 64 >> j
        axis, bit = ("core", 0) if j == 0 else ORDERS[k][j - 1]
        part = pl.ds(BASES[j], half)
        return pltpu.make_async_remote_copy(
            src_ref=sbuf.at[k, part],
            dst_ref=rbuf.at[k, part],
            send_sem=ssem.at[k, j],
            recv_sem=rsem.at[k, j],
            device_id=device_of(flipped(at, axis, bit)),
            device_id_type=MESH,
        )

    core = at["core"]
    for k in range(5):

        def first(c, _, k=k):
            sbuf[k, c] = load(k, chunk_row(ORDERS[k], c, 1 - core)).astype(jnp.bfloat16)
            return 0

        lax.fori_loop(0, 64, first, 0)
        copy(k, 0).start()

    offs = [0] * 5
    for j in range(7):
        for k in range(5):
            half = 64 >> j
            base = BASES[j]
            copy(k, j).wait_recv()
            off = offs[k]

            def add(c, _, k=k, j=j, off=off, base=base):
                got = rbuf[k, base + c].astype(jnp.float32)
                if j == 0:
                    acc[k, c] = load(k, chunk_row(ORDERS[k], c, core)) + got
                else:
                    acc[k, off + c] = acc[k, off + c] + got
                return 0

            lax.fori_loop(0, half, add, 0)
            if j == 6:
                out[k] = acc[k, off]
                continue
            axis, bit = ORDERS[k][j]
            mine = gray(at[axis])[bit]
            nhalf = half // 2
            nbase = BASES[j + 1]
            away = off + (1 - mine) * nhalf
            offs[k] = off + mine * nhalf

            def pack(c, _, k=k, nbase=nbase, away=away):
                sbuf[k, nbase + c] = acc[k, away + c].astype(jnp.bfloat16)
                return 0

            lax.fori_loop(0, nhalf, pack, 0)
            copy(k, j + 1).start()
    for k in range(5):
        for j in range(7):
            copy(k, j).wait_send()


def reduce_scatter(g_key, g_value, g_query, g_out):
    gk = g_key.reshape(128, 8, 2048)
    gv = g_value.reshape(128, 8, 2048)
    gq = g_query.reshape(128, 8, 512)
    go = g_out.reshape(128, 4, 2, 512).transpose(0, 2, 1, 3).reshape(128, 8, 512)
    out = pl.pallas_call(
        reduce_kernel,
        out_shape=jax.ShapeDtypeStruct((5, 16, WIDTH), jnp.float32),
        in_specs=[pl.BlockSpec(memory_space=pltpu.VMEM)] * 4,
        out_specs=pl.BlockSpec(memory_space=pltpu.VMEM),
        scratch_shapes=[
            pltpu.VMEM((5, 127, 16, WIDTH), jnp.bfloat16),
            pltpu.VMEM((5, 127, 16, WIDTH), jnp.bfloat16),
            pltpu.VMEM((5, 64, 16, WIDTH), jnp.float32),
            pltpu.SemaphoreType.DMA((5, 7)),
            pltpu.SemaphoreType.DMA((5, 7)),
        ],
        compiler_params=pltpu.CompilerParams(
            collective_id=0, has_side_effects=True, vmem_limit_bytes=60 * 1024 * 1024
        ),
    )(gk, gv, gq, go)
    key = jnp.concatenate([out[k, :8] for k in range(4)], axis=1)
    value = jnp.concatenate([out[k, 8:] for k in range(4)], axis=1)
    outer = out[4, 8:].reshape(2, 4, 512).transpose(1, 0, 2).reshape(4, 1024)
    return out[4, :8], outer, key, value


def passed_along(value, axis, steps):
    count = lax.axis_size(axis)
    first, last = (max(0, -steps), min(count, count - steps))
    return lax.ppermute(value, axis, [(source, source + steps) for source in range(first, last)])


def attend(query, keys, values, heads):
    size = query.shape[-1] // heads
    scale = size ** (-0.5)
    q_four = query.reshape(query.shape[:-1] + (heads, size))
    k_four = keys.reshape(keys.shape[:-1] + (heads, size))
    v_four = values.reshape(values.shape[:-1] + (heads, size))
    scores = (
        jnp.einsum("bqhd,bkhd->bhqk", q_four, k_four, preferred_element_type=jnp.float32) * scale
    )
    probs = jax.nn.softmax(scores, axis=-1)
    mixed = jnp.einsum(
        "bhqk,bkhd->bqhd", probs.astype(jnp.bfloat16), v_four, preferred_element_type=jnp.float32
    )
    return (mixed.reshape(query.shape), probs)


def attend_back(grad_out, query, keys, values, probs, heads):
    size = query.shape[-1] // heads
    scale = size ** (-0.5)
    g_four = grad_out.reshape(grad_out.shape[:-1] + (heads, size))
    q_four = query.reshape(query.shape[:-1] + (heads, size))
    k_four = keys.reshape(keys.shape[:-1] + (heads, size))
    v_four = values.reshape(values.shape[:-1] + (heads, size))
    weights = probs.astype(jnp.bfloat16)
    d_weights = jnp.einsum("bqhd,bkhd->bhqk", g_four, v_four, preferred_element_type=jnp.float32)
    d_values = jnp.einsum("bhqk,bqhd->bkhd", weights, g_four, preferred_element_type=jnp.float32)
    d_scores = probs * (d_weights - jnp.sum(d_weights * probs, axis=-1, keepdims=True)) * scale
    d_scores = d_scores.astype(jnp.bfloat16)
    d_query = jnp.einsum("bhqk,bkhd->bqhd", d_scores, k_four, preferred_element_type=jnp.float32)
    d_keys = jnp.einsum("bhqk,bqhd->bkhd", d_scores, q_four, preferred_element_type=jnp.float32)
    return (
        d_query.reshape(query.shape),
        d_keys.reshape(keys.shape),
        d_values.reshape(values.shape),
    )


def outer_sum(left, right):
    left_flat = left.reshape(-1, left.shape[-1])
    right_flat = right.reshape(-1, right.shape[-1])
    return lax.dot_general(
        left_flat, right_flat, (((0,), (0,)), ((), ())), preferred_element_type=jnp.float32
    )


def back_project(grad, weight):
    return lax.dot_general(
        grad, weight, (((grad.ndim - 1,), (1,)), ((), ())), preferred_element_type=jnp.float32
    )


def encode(rows, keys, values, gain, w_query, w_out):
    wide = rows.astype(jnp.float32)
    inverse = lax.rsqrt(jnp.mean(wide * wide, axis=-1, keepdims=True) + EPS)
    normed = (wide * inverse * gain).astype(jnp.bfloat16)
    query = jnp.dot(normed, w_query, preferred_element_type=jnp.float32).astype(jnp.bfloat16)
    mixed, probs = attend(query, keys, values, HEADS_E)
    mixed = mixed.astype(jnp.bfloat16)
    encoded = (wide + jnp.dot(mixed, w_out, preferred_element_type=jnp.float32)).astype(
        jnp.bfloat16
    )
    return (encoded, (normed, query, probs, mixed))


def encode_back(grad, keys, values, saved, w_out):
    normed, query, probs, mixed = saved
    g_out = outer_sum(mixed, grad)
    d_mixed = back_project(grad, w_out).astype(jnp.bfloat16)
    d_query, d_keys, d_values = attend_back(d_mixed, query, keys, values, probs, HEADS_E)
    g_query = outer_sum(normed, d_query.astype(jnp.bfloat16))
    return (g_query, g_out, jnp.concatenate([d_keys, d_values], axis=-1).astype(jnp.bfloat16))


def cross_step(span_queries, span_grads, sources, w_key, w_value):
    dec_keys = jnp.dot(sources, w_key, preferred_element_type=jnp.float32).astype(jnp.bfloat16)
    dec_values = jnp.dot(sources, w_value, preferred_element_type=jnp.float32).astype(jnp.bfloat16)
    mixed, probs = attend(span_queries, dec_keys, dec_values, HEADS_D)
    d_query, d_keys, d_values = attend_back(
        span_grads, span_queries, dec_keys, dec_values, probs, HEADS_D
    )
    dk_round = d_keys.astype(jnp.bfloat16)
    dv_round = d_values.astype(jnp.bfloat16)
    grad_sources = (back_project(dk_round, w_key) + back_project(dv_round, w_value)).astype(
        jnp.bfloat16
    )
    return (
        mixed.astype(jnp.bfloat16),
        d_query.astype(jnp.bfloat16),
        grad_sources,
        outer_sum(sources, dk_round),
        outer_sum(sources, dv_round),
    )


def gather_units(database, neighbour_ids, owner_map, units):
    owners = lax.axis_size("enc")
    owner_of = owner_map.reshape(units)
    picked = owner_of[None, :] == jnp.arange(owners, dtype=jnp.int32)[:, None]
    send_ident = jnp.sum(jnp.where(picked, neighbour_ids.reshape(units)[None, :], 0), axis=1)
    got_ident = lax.all_to_all(send_ident, "enc", split_axis=0, concat_axis=0, tiled=True)
    rows = jnp.take(database, got_ident, axis=0)
    got = lax.all_to_all(rows, "enc", split_axis=0, concat_axis=0, tiled=True)
    return jnp.take(got, owner_of, axis=0)


def body(
    queries,
    cond,
    database,
    neighbour_ids,
    owner_map,
    norm_gain,
    w_query_enc,
    w_out_enc,
    w_key_dec,
    w_value_dec,
    cotangent,
):
    spans = queries.shape[0] // SPAN
    half = cond.shape[1] // 2
    both = ("seq", "enc")
    next_queries = passed_along(queries[:SPAN], both, -1)
    next_grads = passed_along(cotangent[:SPAN], both, -1)
    rows = gather_units(database, neighbour_ids, owner_map, spans * NEIGH)
    rows = rows.reshape(spans, NEIGH * NLEN, rows.shape[-1])
    cond_spans = cond.reshape(spans, SPAN, 2 * half)
    keys, values = cond_spans[:, :, :half], cond_spans[:, :, half:]
    sources, saved = encode(rows, keys, values, norm_gain, w_query_enc, w_out_enc)
    span_queries = jnp.concatenate([queries[SPAN:], next_queries]).reshape(spans, SPAN, -1)
    span_grads = jnp.concatenate([cotangent[SPAN:], next_grads]).reshape(spans, SPAN, -1)
    mixed, d_query, grad_sources, g_key, g_value = cross_step(
        span_queries, span_grads, sources, w_key_dec, w_value_dec
    )
    first_mixed = passed_along(mixed[spans - 1], both, 1)
    first_query = passed_along(d_query[spans - 1], both, 1)
    g_query, g_out, cond_grad = encode_back(grad_sources, keys, values, saved, w_out_enc)
    sums = reduce_scatter(g_key, g_value, g_query, g_out)
    attended = jnp.concatenate([first_mixed] + [mixed[c] for c in range(spans - 1)])
    grad_queries = jnp.concatenate([first_query] + [d_query[c] for c in range(spans - 1)])
    return (attended, grad_queries, cond_grad.reshape(cond.shape)) + tuple(sums)


def solution(mesh):
    tokens = P(("seq", "enc"), None)
    return jax.shard_map(
        body,
        mesh=mesh,
        in_specs=(tokens, tokens, P("enc", None, None), tokens, tokens, P(), P(), P(), P(), P(), tokens),
        out_specs=(tokens,) * 7,
        check_vma=False,
    )
```

```python
import functools

import jax
import jax.numpy as jnp
from jax import lax
from jax.experimental import pallas as pl
from jax.experimental.pallas import tpu as pltpu
from jax.sharding import PartitionSpec as P

SPAN = 64
NEIGH = 2
NLEN = 128
EPS = 1e-06
MESH = pl.DeviceIdType.MESH

F32, BF16 = jnp.float32, jnp.bfloat16
AXES = ("x", "y", "z")
TILES = 10
RING = 5
CORE, FIRST, SECOND, THIRD = 0, 64, 112, 124
LATER = (1, 3, 4, 5)


def place():
    s, e = lax.axis_index("seq"), lax.axis_index("enc")
    return dict(core=s % 2, z=(s // 2) % 4, y=(s // 8) * 2 + e % 2, x=e // 2)


def device_of(at):
    y = at["y"]
    return ((y // 2) * 8 + at["z"] * 2 + at["core"], at["x"] * 2 + y % 2)


def moved(at, axis, steps):
    there = dict(at)
    there[axis] = (at[axis] + steps) % (2 if axis == "core" else 4)
    return there


def along(steps):
    p = (lax.axis_index("seq") * 8 + lax.axis_index("enc") + steps) % 128
    return (p // 8, p % 8)


def pick(index, values):
    return jnp.where(index == 0, values[0], jnp.where(index == 1, values[1], values[2]))


def rows_of(axis, v):
    return pick(axis, (2 * v, (v // 2) * 64 + v % 2, 16 * v))


def remote(src, dst, send, recv, device):
    return pltpu.make_async_remote_copy(
        src_ref=src, dst_ref=dst, send_sem=send, recv_sem=recv, device_id=device, device_id_type=MESH
    )


def dot(a, b):
    return jnp.dot(a, b, preferred_element_type=F32)


def dot_nt(a, b):
    return lax.dot_general(a, b, (((1,), (1,)), ((), ())), preferred_element_type=F32)


def dot_tn(a, b):
    return lax.dot_general(a, b, (((0,), (0,)), ((), ())), preferred_element_type=F32)


class Reducer:
    def __init__(self, grads, sbuf, rbuf, acc, acc2, acc3, ssem, rsem, out):
        self.grads, self.sbuf, self.rbuf = grads, sbuf, rbuf
        self.acc, self.acc2, self.acc3 = acc, acc2, acc3
        self.ssem, self.rsem, self.out = ssem, rsem, out
        self.at = place()

    def axes(self, t):
        return [(t + i) % 3 for i in range(3)]

    def mine(self, axis):
        return pick(axis, [self.at[a] for a in AXES])

    def peer(self, axis, r):
        each = [device_of(moved(self.at, a, r)) for a in AXES]
        return tuple(pick(axis, [e[i] for e in each]) for i in (0, 1))

    def copy(self, t, level, r=1):
        if level == 0:
            part, sem, device = pl.ds(0, 64), 0, device_of(moved(self.at, "core", 1))
        else:
            size = (16, 4, 1)[level - 1]
            part = pl.ds((FIRST, SECOND, THIRD)[level - 1] + (r - 1) * size, size)
            sem = 3 * level - 3 + r
            device = self.peer(self.axes(t)[level - 1], r)
        return remote(
            self.sbuf.at[t % RING, part], self.rbuf.at[t, part], self.ssem.at[t, sem], self.rsem.at[t, sem], device
        )

    def rest(self, t):
        _, second, third = self.axes(t)
        return [rows_of(second, i // 4) + rows_of(third, i % 4) for i in range(16)]

    def pack(self, t):
        first = self.axes(t)[0]
        rest = self.rest(t)
        away = 8 * (1 - self.at["core"])

        def some(v, _):
            base = rows_of(first, v) + away
            for i in range(16):
                self.sbuf[t % RING, v * 16 + i] = self.grads[t % 2, base + rest[i]].astype(BF16)
            return 0

        lax.fori_loop(0, 4, some, 0)
        self.copy(t, 0).start()

    def take_core(self, t):
        first = self.axes(t)[0]
        rest = self.rest(t)
        here = 8 * self.at["core"]
        mine = self.mine(first)
        self.copy(t, 0).wait_recv()

        def value(r, i):
            v = (mine + r) % 4
            return self.grads[t % 2, rows_of(first, v) + here + rest[i]] + self.rbuf[t, v * 16 + i].astype(F32)

        for r in (2, 1, 3):
            for i in range(16):
                self.sbuf[t % RING, FIRST + (r - 1) * 16 + i] = value(r, i).astype(BF16)
            self.copy(t, 1, r).start()
        for i in range(16):
            self.acc[t, i] = value(0, i)

    def take_first(self, t):
        mine = self.mine(self.axes(t)[1])
        for r in (1, 2, 3):
            self.copy(t, 1, r).wait_recv()

        def value(r, i):
            c = ((mine + r) % 4) * 4 + i
            got = [self.rbuf[t, FIRST + q * 16 + c].astype(F32) for q in range(3)]
            return self.acc[t, c] + got[0] + got[1] + got[2]

        for r in (2, 1, 3):
            for i in range(4):
                self.sbuf[t % RING, SECOND + (r - 1) * 4 + i] = value(r, i).astype(BF16)
            self.copy(t, 2, r).start()
        for i in range(4):
            self.acc2[t, i] = value(0, i)

    def take_second(self, t):
        mine = self.mine(self.axes(t)[2])
        for r in (1, 2, 3):
            self.copy(t, 2, r).wait_recv()

        def value(r):
            c = (mine + r) % 4
            got = [self.rbuf[t, SECOND + q * 4 + c].astype(F32) for q in range(3)]
            return self.acc2[t, c] + got[0] + got[1] + got[2]

        for r in (2, 1, 3):
            self.sbuf[t % RING, THIRD + r - 1] = value(r).astype(BF16)
            self.copy(t, 3, r).start()
        self.acc3[t] = value(0)

    def take_third(self, t):
        for r in (1, 2, 3):
            self.copy(t, 3, r).wait_recv()
        got = [self.rbuf[t, THIRD + q].astype(F32) for q in range(3)]
        self.out[t] = self.acc3[t] + got[0] + got[1] + got[2]
        self.copy(t, 0).wait_send()
        for level in (1, 2, 3):
            for r in (1, 2, 3):
                self.copy(t, level, r).wait_send()

    def advance(self, s, tiles):
        for later, take in zip(
            LATER[::-1], (self.take_third, self.take_second, self.take_first, self.take_core)
        ):
            t = s - later
            pl.when((t >= 0) & (t < tiles))(functools.partial(take, t))


def by_head(x, reduce, neutral):
    low = lax.broadcasted_iota(jnp.int32, (x.shape[0], 128), 1) < 64
    parts = []
    for t in range(x.shape[1] // 128):
        one = x[:, t * 128 : t * 128 + 128]
        left = reduce(jnp.where(low, one, neutral), axis=-1, keepdims=True)
        right = reduce(jnp.where(low, neutral, one), axis=-1, keepdims=True)
        parts.append(jnp.where(low, left, right))
    return jnp.concatenate(parts, axis=1)


def head_blocks(x):
    wide = x.astype(F32)
    head = lax.broadcasted_iota(jnp.int32, x.shape, 1) // 64
    return jnp.concatenate([jnp.where(head == h, wide, 0.0) for h in range(4)], axis=0).astype(BF16)


def head_diagonal(x):
    head = lax.broadcasted_iota(jnp.int32, (64, 256), 1) // 64
    return sum(jnp.where(head == h, x[h * 64 : h * 64 + 64], 0.0) for h in range(4))


def two_heads(x):
    none = jnp.zeros((x.shape[0], 128), x.dtype)
    return jnp.concatenate(
        [jnp.concatenate([x[:, :128], none], axis=1), jnp.concatenate([none, x[:, 128:]], axis=1)], axis=0
    )


def own_heads(x):
    return jnp.concatenate([x[:64, :128], x[64:, 128:]], axis=1)


def main_kernel(
    rows, cond, gain, wq, wo, wk, wv, q_ref, g_ref,
    att, dq_out, dcond, sums,
    normed, query, probs, mixed, src, keys, vals, dk_all, dv_all, ge, dmix, last, first,
    grads, sbuf, rbuf, acc, acc2, acc3, ssem, rsem, shift_s, shift_r,
):
    red = Reducer(grads, sbuf, rbuf, acc, acc2, acc3, ssem, rsem, sums)
    at = red.at
    barrier = pltpu.get_barrier_semaphore()
    peers = [device_of(moved(at, "core", 1))]
    peers += [device_of(moved(at, a, r)) for a in AXES for r in (1, 2, 3)]
    for peer in peers + [along(-1)]:
        pl.semaphore_signal(barrier, inc=1, device_id=peer, device_id_type=MESH)
    pl.semaphore_wait(barrier, len(peers) + 1)

    def encode(s, _):
        here = pl.ds(pl.multiple_of(s * 256, 256), 256)
        span = pl.ds(pl.multiple_of(s * 64, 64), 64)
        wide = rows[here, :].astype(F32)
        inverse = lax.rsqrt(jnp.mean(wide * wide, axis=-1, keepdims=True) + EPS)
        normed[here, :] = (wide * inverse * gain[...]).astype(BF16)
        query[here, :] = dot(normed[here, :], wq[...]).astype(BF16)
        for half in range(2):
            cols = slice(half * 256, half * 256 + 256)
            k4 = head_blocks(cond[span, cols])
            v4 = head_blocks(cond[span, 512 + half * 256 : 768 + half * 256])
            scores = dot_nt(query[here, cols], k4) * 0.125
            e = jnp.exp(scores - by_head(scores, jnp.max, -jnp.inf))
            p = e / by_head(e, jnp.sum, 0.0)
            probs[here, cols] = p
            mixed[here, cols] = dot(p.astype(BF16), v4).astype(BF16)
        src[here, :] = (rows[here, :].astype(F32) + dot(mixed[here, :], wo[...])).astype(BF16)
        return 0

    lax.fori_loop(0, 3, encode, 0)

    scale = 128 ** (-0.5)

    def decode(t, _):
        cols = pl.ds(pl.multiple_of(t * 256, 256), 256)
        keys[...] = dot(src[...], wk[:, cols]).astype(BF16)
        vals[...] = dot(src[...], wv[:, cols]).astype(BF16)
        for s in range(3):
            here = slice(s * 256, s * 256 + 256)
            span = slice(s * 64, s * 64 + 64)
            q2, g2 = two_heads(q_ref[span, cols]), two_heads(g_ref[span, cols])
            k, v = keys[here, :], vals[here, :]
            scores = dot_nt(q2, k) * scale
            e = jnp.exp(scores - jnp.max(scores, axis=-1, keepdims=True))
            p = e / jnp.sum(e, axis=-1, keepdims=True)
            w = p.astype(BF16)
            o = own_heads(dot(w, v)).astype(BF16)
            dw = dot_nt(g2, v)
            ds = (p * (dw - jnp.sum(dw * p, axis=-1, keepdims=True)) * scale).astype(BF16)
            dq = own_heads(dot(ds, k)).astype(BF16)
            if s < 2:
                after = slice(s * 64 + 64, s * 64 + 128)
                att[after, cols] = o
                dq_out[after, cols] = dq
            else:
                last[0, :, cols] = o
                last[1, :, cols] = dq
            dk_all[here, cols] = dot_tn(ds, q2).astype(BF16)
            dv_all[here, cols] = dot_tn(w, g2).astype(BF16)
        grads[t % 2, :, :8] = dot_tn(src[...], dk_all[:, cols]).reshape(128, 8, 256)
        grads[t % 2, :, 8:] = dot_tn(src[...], dv_all[:, cols]).reshape(128, 8, 256)
        red.advance(t, 8)
        red.pack(t)
        return 0

    lax.fori_loop(0, 8, decode, 0)
    shift = remote(last, first, shift_s, shift_r, along(1))
    shift.start()

    def sources_back(i, _):
        cols = pl.ds(pl.multiple_of(i * 256, 256), 256)
        ge[:, cols] = (dot_nt(dk_all[...], wk[cols, :]) + dot_nt(dv_all[...], wv[cols, :])).astype(BF16)
        red.advance(i + 8, 8)
        return 0

    lax.fori_loop(0, 4, sources_back, 0)

    def outer_out(i, _):
        cols = pl.ds(pl.multiple_of(i * 256, 256), 256)
        sheet = dot_tn(mixed[...], ge[:, cols])
        for upper in range(2):
            part = sheet.reshape(64, 8, 256)[:, upper * 4 : upper * 4 + 4]
            for j in range(4):
                pl.when(i == j)(functools.partial(put_out, part, upper, j))
        return 0

    def put_out(part, upper, j):
        grads_out = grads.at[0]
        for q in range(64):
            grads_out[2 * q + upper, j * 4 : j * 4 + 4, :] = part[q]

    lax.fori_loop(0, 4, outer_out, 0)
    red.take_third(7)
    red.pack(8)
    dmix[...] = dot_nt(ge[...], wo[...]).astype(BF16)

    def encode_back(s, _):
        here = pl.ds(pl.multiple_of(s * 256, 256), 256)
        span = pl.ds(pl.multiple_of(s * 64, 64), 64)
        for half in range(2):
            cols = slice(half * 256, half * 256 + 256)
            vcols = slice(512 + half * 256, 768 + half * 256)
            k4, v4 = head_blocks(cond[span, cols]), head_blocks(cond[span, vcols])
            p = probs[here, cols]
            g = dmix[here, cols]
            q = query[here, cols]
            dw = dot_nt(g, v4)
            ds = (p * (dw - by_head(dw * p, jnp.sum, 0.0)) * 0.125).astype(BF16)
            dcond[span, vcols] = head_diagonal(dot_tn(p.astype(BF16), g)).astype(BF16)
            dcond[span, cols] = head_diagonal(dot_tn(ds, q)).astype(BF16)
            query[here, cols] = dot(ds, k4).astype(BF16)
        return 0

    lax.fori_loop(0, 3, encode_back, 0)
    red.take_core(8)
    for half in range(2):
        cols = slice(half * 256, half * 256 + 256)
        sheet = dot_tn(normed[...], query[:, cols])
        grads[1, :, half * 8 : half * 8 + 8] = sheet.reshape(128, 8, 256)
    red.pack(9)
    red.take_first(8)
    red.take_core(9)
    red.take_second(8)
    shift.wait()
    kept = jnp.where(lax.axis_index("seq") + lax.axis_index("enc") == 0, 0.0, 1.0).astype(BF16)
    att[:64, :] = first[0] * kept
    dq_out[:64, :] = first[1] * kept
    red.take_third(8)
    red.take_first(9)
    red.take_second(9)
    red.take_third(9)


def fused(rows, cond, gain, wq, wo, wk, wv, queries, grads):
    vmem = pl.BlockSpec(memory_space=pltpu.VMEM)
    shape = jax.ShapeDtypeStruct
    dma = pltpu.SemaphoreType.DMA
    out = pl.pallas_call(
        main_kernel,
        out_shape=(
            shape((192, 2048), BF16),
            shape((192, 2048), BF16),
            shape((192, 1024), BF16),
            shape((TILES, 16, 256), F32),
        ),
        in_specs=[vmem] * 9,
        out_specs=(vmem,) * 4,
        scratch_shapes=[
            pltpu.VMEM((768, 1024), BF16),
            pltpu.VMEM((768, 512), BF16),
            pltpu.VMEM((768, 512), F32),
            pltpu.VMEM((768, 512), BF16),
            pltpu.VMEM((768, 1024), BF16),
            pltpu.VMEM((768, 256), BF16),
            pltpu.VMEM((768, 256), BF16),
            pltpu.VMEM((768, 2048), BF16),
            pltpu.VMEM((768, 2048), BF16),
            pltpu.VMEM((768, 1024), BF16),
            pltpu.VMEM((768, 512), BF16),
            pltpu.VMEM((2, 64, 2048), BF16),
            pltpu.VMEM((2, 64, 2048), BF16),
            pltpu.VMEM((2, 128, 16, 256), F32),
            pltpu.VMEM((RING, 127, 16, 256), BF16),
            pltpu.VMEM((TILES, 127, 16, 256), BF16),
            pltpu.VMEM((TILES, 16, 16, 256), F32),
            pltpu.VMEM((TILES, 4, 16, 256), F32),
            pltpu.VMEM((TILES, 16, 256), F32),
            dma((TILES, 10)),
            dma((TILES, 10)),
            dma,
            dma,
        ],
        compiler_params=pltpu.CompilerParams(
            collective_id=0, has_side_effects=True, vmem_limit_bytes=62 * 1024 * 1024
        ),
    )(rows, cond, gain, wq, wo, wk, wv, queries, grads)
    attended, grad_queries, grad_cond, sums = out
    key = jnp.concatenate([sums[t, :8] for t in range(8)], axis=1)
    value = jnp.concatenate([sums[t, 8:] for t in range(8)], axis=1)
    outer = sums[8].reshape(4, 4, 256).transpose(1, 0, 2).reshape(4, 1024)
    query = jnp.concatenate([sums[9, :8], sums[9, 8:]], axis=1)
    return attended, grad_queries, grad_cond, query, outer, key, value


def passed_along(value, axis, steps):
    count = lax.axis_size(axis)
    first, last = (max(0, -steps), min(count, count - steps))
    return lax.ppermute(value, axis, [(source, source + steps) for source in range(first, last)])


def gather_units(database, neighbour_ids, owner_map, units):
    owners = lax.axis_size("enc")
    owner_of = owner_map.reshape(units)
    picked = owner_of[None, :] == jnp.arange(owners, dtype=jnp.int32)[:, None]
    send_ident = jnp.sum(jnp.where(picked, neighbour_ids.reshape(units)[None, :], 0), axis=1)
    got_ident = lax.all_to_all(send_ident, "enc", split_axis=0, concat_axis=0, tiled=True)
    rows = jnp.take(database, got_ident, axis=0)
    got = lax.all_to_all(rows, "enc", split_axis=0, concat_axis=0, tiled=True)
    return jnp.take(got, owner_of, axis=0)


def body(
    queries,
    cond,
    database,
    neighbour_ids,
    owner_map,
    norm_gain,
    w_query_enc,
    w_out_enc,
    w_key_dec,
    w_value_dec,
    cotangent,
):
    units = neighbour_ids.shape[0] * NEIGH
    both = ("seq", "enc")
    next_queries = passed_along(queries[:SPAN], both, -1)
    next_grads = passed_along(cotangent[:SPAN], both, -1)
    rows = gather_units(database, neighbour_ids, owner_map, units).reshape(units * NLEN, -1)
    span_queries = jnp.concatenate([queries[SPAN:], next_queries])
    span_grads = jnp.concatenate([cotangent[SPAN:], next_grads])
    return fused(
        rows, cond, norm_gain.reshape(1, -1), w_query_enc, w_out_enc, w_key_dec, w_value_dec, span_queries, span_grads
    )


def solution(mesh):
    tokens = P(("seq", "enc"), None)
    return jax.shard_map(
        body,
        mesh=mesh,
        in_specs=(tokens, tokens, P("enc", None, None), tokens, tokens, P(), P(), P(), P(), P(), tokens),
        out_specs=(tokens,) * 7,
        check_vma=False,
    )
```

```python
import functools

import jax
import jax.numpy as jnp
from jax import lax
from jax.experimental import pallas as pl
from jax.experimental.pallas import tpu as pltpu
from jax.sharding import PartitionSpec as P

EPS = 1e-06
MESH = pl.DeviceIdType.MESH

F32, BF16 = jnp.float32, jnp.bfloat16
AXES = ("x", "y", "z")
TILES = 9
SERVERS = ((0, 0), (0, 1), (1, 0), (1, -1), (2, 0), (2, 1), (3, 0), (3, -1))


def place():
    s, e = lax.axis_index("seq"), lax.axis_index("enc")
    return dict(core=s % 2, z=(s // 2) % 4, y=(s // 8) * 2 + e % 2, x=e // 2)


def device_of(at):
    y = at["y"]
    return ((y // 2) * 8 + at["z"] * 2 + at["core"], at["x"] * 2 + y % 2)


def moved(at, **steps):
    there = dict(at)
    for axis, step in steps.items():
        there[axis] = (at[axis] + step) % (2 if axis == "core" else 4)
    return there


def along(steps):
    p = (lax.axis_index("seq") * 8 + lax.axis_index("enc") + steps) % 128
    return (p // 8, p % 8)


def pick(index, values):
    if isinstance(index, int):
        return values[index]
    return jnp.where(index == 0, values[0], jnp.where(index == 1, values[1], values[2]))


def rows_of(axis, v):
    return ((0, 2 * v), (v // 2 * 4, v % 2), (v, 0))[axis]


def pick_pair(index, pairs):
    return tuple(pick(index, [pair[i] for pair in pairs]) for i in (0, 1))


class Map:
    def __init__(self):
        at = self.at = place()
        self.core = at["core"]
        self.other_core = device_of(moved(at, core=1))
        self.devices = [[device_of(moved(at, **{a: r})) for a in AXES] for r in range(4)]
        self.values = [[(at[a] + r) % 4 for a in AXES] for r in range(4)]
        self.places = [[rows_of(i, each[i]) for i in range(3)] for each in self.values]
        self.before, self.after = along(-1), along(1)


def remote(src, dst, send, recv, device):
    return pltpu.make_async_remote_copy(
        src_ref=src, dst_ref=dst, send_sem=send, recv_sem=recv, device_id=device, device_id_type=MESH
    )


def dot(a, b):
    return jnp.dot(a, b, preferred_element_type=F32)


def dot_nt(a, b):
    return lax.dot_general(a, b, (((1,), (1,)), ((), ())), preferred_element_type=F32)


def dot_tn(a, b):
    return lax.dot_general(a, b, (((0,), (0,)), ((), ())), preferred_element_type=F32)


class Tile:
    def __init__(self, map, t, turn, grads, came, sends, gets, kept, ssem, rsem, put):
        self.map, self.t, self.grads, self.came = map, t, grads, came
        self.sends, self.gets, self.kept = sends, gets, kept
        self.ssem, self.rsem, self.put = ssem, rsem, put
        if isinstance(turn, int):
            self.axes = [(turn + i) % 3 for i in range(3)]
        else:
            self.axes = [turn, jnp.where(turn == 2, 0, turn + 1), jnp.where(turn == 0, 2, turn - 1)]

    def value(self, level, r):
        return pick(self.axes[level], self.map.values[r])

    def copy(self, level, r=1):
        if level == 0:
            device, src, dst, sem = self.map.other_core, self.outgoing(), self.came, 0
        else:
            device = pick_pair(self.axes[level - 1], self.map.devices[r])
            src, dst, sem = self.sends[level - 1].at[r - 1], self.gets[level - 1].at[r - 1], 3 * level - 3 + r
        return remote(src, dst, self.ssem.at[self.t, sem], self.rsem.at[self.t, sem], device)

    def start(self):
        self.copy(0).start()

    def take(self, level):
        if level == 0:
            self.copy(0).wait_recv()
        else:
            for r in (1, 2, 3):
                self.copy(level, r).wait_recv()
        (self.take_core, self.take_first, self.take_second, self.take_third)[level]()

    def take_core(self):
        each = [
            [pick_pair(self.axes[level], [rows_of(a, v) for a in range(3)]) for v in range(4)] for level in (1, 2)
        ]
        rest = [tuple(a + b for a, b in zip(each[0][i // 4], each[1][i % 4])) for i in range(16)]
        for r in (2, 1, 3, 0):
            high, low = pick_pair(self.axes[0], self.map.places[r])
            for i in range(16):
                value = self.pair(high + rest[i][0], low + rest[i][1])
                if r:
                    self.sends[0][r - 1, i] = self.lower(value)
                else:
                    self.kept[0][i] = value
            if r:
                self.copy(1, r).start()
        self.copy(0).wait_send()

    def take_first(self):
        for r in (2, 1, 3, 0):
            first = self.value(1, r) * 4
            for i in range(4):
                c = first + i
                got = [self.higher(self.gets[0][q, c]) for q in range(3)]
                value = self.kept[0][c] + got[0] + got[1] + got[2]
                if r:
                    self.sends[1][r - 1, i] = value.astype(self.sends[1].dtype)
                else:
                    self.kept[1][i] = value
            if r:
                self.copy(2, r).start()

    def take_second(self):
        for r in (2, 1, 3, 0):
            c = self.value(2, r)
            got = [self.gets[1][q, c].astype(F32) for q in range(3)]
            value = self.kept[1][c] + got[0] + got[1] + got[2]
            if r:
                self.sends[2][r - 1, 0] = value.astype(self.sends[2].dtype)
                self.copy(3, r).start()
            else:
                self.kept[2][0] = value

    def take_third(self):
        got = [self.gets[2][q, 0].astype(F32) for q in range(3)]
        self.put(self.kept[2][0] + got[0] + got[1] + got[2])
        for level in (1, 2, 3):
            for r in (1, 2, 3):
                self.copy(level, r).wait_send()


class PairTile(Tile):
    def outgoing(self):
        return self.grads.at[:, :, 1 - self.map.core]

    def pair(self, high, low):
        core = self.map.core
        parts = [self.grads[i, high, core, low] + self.came[i, high, low] for i in (0, 1)]
        return jnp.concatenate(parts, axis=0)

    def lower(self, value):
        return value.astype(BF16)

    def higher(self, value):
        return value.astype(F32)


class HalfTile(Tile):
    def outgoing(self):
        return self.grads.at[:, 1 - self.map.core]

    def pair(self, high, low):
        return self.grads[high, self.map.core, low] + self.came[high, low]

    def lower(self, value):
        return jnp.concatenate([value[:, :128], value[:, 128:]], axis=0).astype(BF16)

    def higher(self, value):
        wide = value.astype(F32)
        return jnp.concatenate([wide[:8], wide[8:]], axis=1)


def by_head(x, reduce, neutral):
    low = lax.broadcasted_iota(jnp.int32, (x.shape[0], 128), 1) < 64
    parts = []
    for t in range(x.shape[1] // 128):
        one = x[:, t * 128 : t * 128 + 128]
        left = reduce(jnp.where(low, one, neutral), axis=-1, keepdims=True)
        right = reduce(jnp.where(low, neutral, one), axis=-1, keepdims=True)
        parts.append(jnp.where(low, left, right))
    return jnp.concatenate(parts, axis=1)


def head_blocks(x):
    wide = x.astype(F32)
    head = lax.broadcasted_iota(jnp.int32, x.shape, 1) // 64
    return jnp.concatenate([jnp.where(head == h, wide, 0.0) for h in range(4)], axis=0).astype(BF16)


def head_diagonal(x):
    head = lax.broadcasted_iota(jnp.int32, (64, 256), 1) // 64
    return sum(jnp.where(head == h, x[h * 64 : h * 64 + 64], 0.0) for h in range(4))


def two_heads(x):
    none = jnp.zeros((x.shape[0], 128), x.dtype)
    return jnp.concatenate(
        [jnp.concatenate([x[:, :128], none], axis=1), jnp.concatenate([none, x[:, 128:]], axis=1)], axis=0
    )


def own_heads(x):
    return jnp.concatenate([x[:64, :128], x[64:, 128:]], axis=1)


def main_kernel(
    codes, database, cond_in, gain, wq_in, wo_in, wk_in, wv_in, q_in, g_in,
    att, dq_out, dcond, gq_out, go_out, gk_out, gv_out,
    pool, cond, wq, wo, wk, wv, q_ref, g_ref,
    asked, asks, blocks_out, blocks, later,
    normed, query, probs, mixed, src, keys, vals, dmix, last, first,
    grads, came, send1, get1, send2, get2, send3, get3, kept1, kept2, kept3,
    hcame, hsend1, hget1, hsend2, hget2, hsend3, hget3, hkept1, hkept2, hkept3,
    load_sem, ask_s, ask_r, block_s, block_r, ahead_s, ahead_r, shift_s, shift_r, ssem, rsem,
):
    map = Map()
    at = map.at
    me = lax.axis_index("seq") * 8 + lax.axis_index("enc")
    loads = [
        pltpu.make_async_copy(a, b, load_sem.at[i])
        for i, (a, b) in enumerate(
            (
                (database, pool), (cond_in, cond), (wq_in, wq), (wo_in, wo),
                (wk_in, wk), (wv_in, wv), (q_in, q_ref), (g_in, g_ref),
            )
        )
    ]
    loads[0].start()

    barrier = pltpu.get_barrier_semaphore()
    steps = {(dx * s % 4, dy * s % 4) for dx, dy in SERVERS for s in (1, -1)} | {(0, 2)}
    steps = sorted(steps - {(0, 0)})
    peers = [device_of(moved(at, x=dx, y=dy)) for dx, dy in steps]
    peers += [device_of(moved(at, core=1))] + [device_of(moved(at, z=r)) for r in (1, 2, 3)]
    peers += [map.before, map.after]
    for peer in peers:
        pl.semaphore_signal(barrier, inc=1, device_id=peer, device_id_type=MESH)
    pl.semaphore_wait(barrier, len(peers))

    first_row = [
        (((at["x"] + dx) % 4) * 2 + (at["y"] + dy) % 2) * 32 for dx, dy in SERVERS
    ]

    def served(code, r):
        return (code >= first_row[r]) & (code < first_row[r] + 32)

    def row_at(r):
        each = [codes[s, j] for s in range(3) for j in range(2)]
        return sum(jnp.where(served(code, r), code - first_row[r], 0) for code in each)

    asking, answers = [], []
    for r in (5, 7, 3, 4, 2, 6, 1):
        dx, dy = SERVERS[r]
        asks[r] = jnp.full((8, 128), row_at(r), jnp.int32)
        copy = remote(
            asks.at[r], asked.at[r], ask_s.at[r], ask_r.at[r], device_of(moved(at, x=dx, y=dy))
        )
        copy.start()
        asking.append((r, copy))
    for copy in loads[1:]:
        copy.start()
    loads[0].wait()
    for r, copy in asking:
        dx, dy = SERVERS[r]
        copy.wait_recv()
        blocks_out[r] = pool[jnp.max(asked[r])]
        answer = remote(
            blocks_out.at[r], blocks.at[r], block_s.at[r], block_r.at[r], device_of(moved(at, x=-dx, y=-dy))
        )
        answer.start()
        answers.append(answer)
    blocks[0] = pool[row_at(0)]
    for r, copy in asking:
        copy.wait_send()
    for copy in loads[1:4]:
        copy.wait()
    for answer in answers:
        answer.wait_recv()

    def encode(s, _):
        here = pl.ds(pl.multiple_of(s * 256, 256), 256)
        span = pl.ds(pl.multiple_of(s * 64, 64), 64)

        def wide():
            parts = []
            for j in range(2):
                code = codes[s, j]
                parts.append(blocks[sum(jnp.where(served(code, r), r, 0) for r in range(1, 8))])
            return jnp.concatenate(parts, axis=0).astype(F32)

        raw = wide()
        inverse = lax.rsqrt(jnp.mean(raw * raw, axis=-1, keepdims=True) + EPS)
        normed[here, :] = (raw * inverse * gain[...]).astype(BF16)
        query[here, :] = dot(normed[here, :], wq[...]).astype(BF16)
        for half in range(2):
            cols = slice(half * 256, half * 256 + 256)
            k4 = head_blocks(cond[span, cols])
            v4 = head_blocks(cond[span, 512 + half * 256 : 768 + half * 256])
            scores = dot_nt(query[here, cols], k4) * 0.125
            e = jnp.exp(scores - by_head(scores, jnp.max, -jnp.inf))
            p = e / by_head(e, jnp.sum, 0.0)
            probs[here, cols] = p
            mixed[here, cols] = dot(p.astype(BF16), v4).astype(BF16)
        src[here, :] = (wide() + dot(mixed[here, :], wo[...])).astype(BF16)
        return 0

    def ahead(t):
        cols = pl.ds(pl.multiple_of(t * 256, 256), 256)
        return [
            remote(
                ref.at[pl.ds(0, 64), cols], later.at[i, :, cols], ahead_s.at[i, t], ahead_r.at[i, t], map.before
            )
            for i, ref in enumerate((q_in, g_in))
        ]

    def send_ahead(t, _):
        for copy in ahead(t):
            copy.start()
        return 0

    lax.fori_loop(0, 8, send_ahead, 0)
    lax.fori_loop(0, 3, encode, 0)
    for copy in loads[4:]:
        copy.wait()
    for answer in answers:
        answer.wait_send()
    followed = jnp.where(me == 127, 0.0, 1.0).astype(BF16)

    def whole_tile(t):
        def put(total):
            if isinstance(t, int) and t == 8:
                for j in range(4):
                    go_out[:, j * 256 : j * 256 + 256] = total[j * 4 : j * 4 + 4]
                return
            cols = pl.ds(t * 256, 256) if isinstance(t, int) else pl.ds(pl.multiple_of(t * 256, 256), 256)
            gk_out[:, cols] = total[:8]
            gv_out[:, cols] = total[8:]

        turn = t % 3
        return PairTile(
            map, t, turn, grads.at[turn], came.at[t % 4],
            (send1.at[t], send2.at[t], send3.at[t]), (get1.at[t], get2.at[t], get3.at[t]),
            (kept1.at[t], kept2.at[t], kept3.at[t]), ssem, rsem, put,
        )

    def half_tile(i):
        def put(total):
            gq_out[:, i * 256 : i * 256 + 256] = total

        return HalfTile(
            map, TILES + i, i + 1, grads.at[0, i], hcame.at[i],
            (hsend1.at[i], hsend2.at[i], hsend3.at[i]), (hget1.at[i], hget2.at[i], hget3.at[i]),
            (hkept1.at[i], hkept2.at[i], hkept3.at[i]), ssem, rsem, put,
        )

    def take(level, t):
        whole_tile(t).take(level)

    scale = 128 ** (-0.5)

    def half_rows(t):
        return t // 4 * 6, pl.ds(pl.multiple_of(t % 4 * 256, 256), 256)

    def decode(t, _):
        cols = pl.ds(pl.multiple_of(t * 256, 256), 256)
        base, pool_cols = half_rows(t)
        for copy in ahead(t):
            copy.wait()
        keys[...] = dot(src[...], wk[:, cols]).astype(BF16)
        vals[...] = dot(src[...], wv[:, cols]).astype(BF16)
        for s in range(3):
            here = slice(s * 256, s * 256 + 256)
            after = slice(s * 64 + 64, s * 64 + 128)
            if s < 2:
                q2, g2 = two_heads(q_ref[after, cols]), two_heads(g_ref[after, cols])
            else:
                q2, g2 = (two_heads(later[i, :, cols] * followed) for i in (0, 1))
            k, v = keys[here, :], vals[here, :]
            scores = dot_nt(q2, k) * scale
            e = jnp.exp(scores - jnp.max(scores, axis=-1, keepdims=True))
            p = e / jnp.sum(e, axis=-1, keepdims=True)
            w = p.astype(BF16)
            o = own_heads(dot(w, v)).astype(BF16)
            dw = dot_nt(g2, v)
            ds = (p * (dw - jnp.sum(dw * p, axis=-1, keepdims=True)) * scale).astype(BF16)
            dq = own_heads(dot(ds, k)).astype(BF16)
            if s < 2:
                att[after, cols] = o
                dq_out[after, cols] = dq
            else:
                last[0, :, cols] = o
                last[1, :, cols] = dq
            low = base + s * 2
            pool[pl.ds(low, 2), :, pool_cols] = dot_tn(ds, q2).astype(BF16).reshape(2, 128, 256)
            pool[pl.ds(low + 12, 2), :, pool_cols] = dot_tn(w, g2).astype(BF16).reshape(2, 128, 256)
        for i in range(2):
            sheet = dot_tn(src[...], pool[pl.ds(base + 12 * i, 6), :, pool_cols].reshape(768, 256))
            grads[t % 3, i] = sheet.reshape(8, 2, 8, 8, 256)
        for level, behind in ((2, 7), (1, 5), (0, 2)):
            pl.when(t >= behind)(functools.partial(take, level, t - behind))
        whole_tile(t).start()
        return 0

    lax.fori_loop(0, 8, decode, 0)
    shift = remote(last, first, shift_s, shift_r, map.after)
    shift.start()

    points = (((1, 3), (2, 1)), ((0, 6), (3, 0)), ((0, 7), (1, 4)), ((2, 2), (3, 1)))
    for i, point in enumerate(points):
        cols = slice(i * 256, i * 256 + 256)
        total = sum(
            dot_nt(pool[j * 6 : j * 6 + 6].reshape(768, 1024), w[cols, j % 2 * 1024 : j % 2 * 1024 + 1024])
            for j, w in enumerate((wk, wk, wv, wv))
        )
        pool[24:30, :, cols] = total.astype(BF16).reshape(6, 128, 256)
        for level, t in point:
            take(level, t)
    for j in range(4):
        sheet = dot_tn(mixed[...], pool[24:30, :, j * 256 : j * 256 + 256].reshape(768, 256)).reshape(64, 8, 256)
        for p in range(128):
            part = sheet[p // 2, p % 2 * 4 : p % 2 * 4 + 4]
            grads[2, j // 2, p // 16, p // 8 % 2, p % 8, j % 2 * 4 : j % 2 * 4 + 4, :] = part
    whole_tile(8).start()
    take(1, 5)
    take(2, 3)
    dmix[...] = dot_nt(pool[24:30].reshape(768, 1024), wo[...]).astype(BF16)
    for level, t in ((3, 2), (2, 4)):
        take(level, t)

    dquery = (keys, vals)
    for half in range(2):
        cols = slice(half * 256, half * 256 + 256)
        vcols = slice(512 + half * 256, 768 + half * 256)

        def query_back(s, _, half=half, cols=cols, vcols=vcols):
            here = pl.ds(pl.multiple_of(s * 256, 256), 256)
            span = pl.ds(pl.multiple_of(s * 64, 64), 64)
            k4, v4 = head_blocks(cond[span, cols]), head_blocks(cond[span, vcols])
            p = probs[here, cols]
            dw = dot_nt(dmix[here, cols], v4)
            ds = (p * (dw - by_head(dw * p, jnp.sum, 0.0)) * 0.125).astype(BF16)
            mixed[here, cols] = ds
            dquery[half][here, :] = dot(ds, k4).astype(BF16)
            return 0

        def cond_back(s, _, cols=cols, vcols=vcols):
            here = pl.ds(pl.multiple_of(s * 256, 256), 256)
            span = pl.ds(pl.multiple_of(s * 64, 64), 64)
            w = probs[here, cols].astype(BF16)
            dcond[span, vcols] = head_diagonal(dot_tn(w, dmix[here, cols])).astype(BF16)
            dcond[span, cols] = head_diagonal(dot_tn(mixed[here, cols], query[here, cols])).astype(BF16)
            return 0

        lax.fori_loop(0, 3, query_back, 0)
        grads[0, half] = dot_tn(normed[...], dquery[half][...]).reshape(8, 2, 8, 8, 256)
        half_tile(half).start()
        if half == 0:
            for level, t in ((1, 6), (0, 8), (3, 3)):
                take(level, t)
        else:
            for level, t in ((1, 7), (2, 5)):
                take(level, t)
            half_tile(0).take(0)
        lax.fori_loop(0, 3, cond_back, 0)
    half_tile(1).take(0)
    for level, t in ((3, 4), (2, 6), (3, 5), (2, 7), (1, 8)):
        take(level, t)
    half_tile(0).take(1)
    shift.wait()
    followed = jnp.where(me == 0, 0.0, 1.0).astype(BF16)
    att[:64, :] = first[0] * followed
    dq_out[:64, :] = first[1] * followed
    half_tile(1).take(1)
    for level, t in ((3, 6), (3, 7), (2, 8)):
        take(level, t)
    half_tile(0).take(2)
    half_tile(1).take(2)
    take(3, 8)
    half_tile(0).take(3)
    half_tile(1).take(3)


def fused(codes, database, cond, gain, wq, wo, wk, wv, queries, grads):
    vmem, smem = pl.BlockSpec(memory_space=pltpu.VMEM), pl.BlockSpec(memory_space=pltpu.SMEM)
    hbm = pl.BlockSpec(memory_space=pl.ANY)
    shape, dma = jax.ShapeDtypeStruct, pltpu.SemaphoreType.DMA
    half = lambda *dims: pltpu.VMEM(dims, BF16)
    full = lambda *dims: pltpu.VMEM(dims, F32)
    outs = pl.pallas_call(
        main_kernel,
        out_shape=(
            shape((192, 2048), BF16),
            shape((192, 2048), BF16),
            shape((192, 1024), BF16),
            shape((8, 512), F32),
            shape((4, 1024), F32),
            shape((8, 2048), F32),
            shape((8, 2048), F32),
        ),
        in_specs=[smem, hbm, hbm, vmem] + [hbm] * 6,
        out_specs=(vmem,) * 7,
        scratch_shapes=[
            half(32, 128, 1024), half(192, 1024), half(1024, 512), half(512, 1024),
            half(1024, 2048), half(1024, 2048), half(192, 2048), half(192, 2048),
            pltpu.VMEM((8, 8, 128), jnp.int32), pltpu.VMEM((8, 8, 128), jnp.int32),
            half(8, 128, 1024), half(8, 128, 1024), half(2, 64, 2048),
            half(768, 1024), half(768, 512), full(768, 512), half(768, 512), half(768, 1024),
            half(768, 256), half(768, 256), half(768, 512),
            half(2, 64, 2048), half(2, 64, 2048),
            full(3, 2, 8, 2, 8, 8, 256), full(4, 2, 8, 8, 8, 256),
            half(TILES, 3, 16, 16, 256), half(TILES, 3, 16, 16, 256),
            half(TILES, 3, 4, 16, 256), half(TILES, 3, 4, 16, 256),
            half(TILES, 3, 1, 16, 256), half(TILES, 3, 1, 16, 256),
            full(TILES, 16, 16, 256), full(TILES, 4, 16, 256), full(TILES, 1, 16, 256),
            full(2, 8, 8, 8, 256), half(2, 3, 16, 16, 128), half(2, 3, 16, 16, 128),
            full(2, 3, 4, 8, 256), full(2, 3, 4, 8, 256), full(2, 3, 1, 8, 256), full(2, 3, 1, 8, 256),
            full(2, 16, 8, 256), full(2, 4, 8, 256), full(2, 1, 8, 256),
            dma((8,)), dma((8,)), dma((8,)), dma((8,)), dma((8,)), dma((2, 8)), dma((2, 8)), dma, dma,
            dma((TILES + 2, 10)), dma((TILES + 2, 10)),
        ],
        compiler_params=pltpu.CompilerParams(
            collective_id=0, has_side_effects=True, vmem_limit_bytes=63 * 1024 * 1024
        ),
    )(codes, database, cond, gain, wq, wo, wk, wv, queries, grads)

    def leave(*refs):
        n, sem = len(outs), refs[-1]
        copies = [pltpu.make_async_copy(refs[i], refs[n + i], sem.at[i]) for i in range(n)]
        for copy in copies:
            copy.start()
        for copy in copies:
            copy.wait()

    return pl.pallas_call(
        leave,
        out_shape=tuple(shape(o.shape, o.dtype) for o in outs),
        in_specs=[hbm] * len(outs),
        out_specs=(vmem,) * len(outs),
        scratch_shapes=[dma((len(outs),))],
    )(*outs)


def body(
    queries,
    cond,
    database,
    neighbour_ids,
    owner_map,
    norm_gain,
    w_query_enc,
    w_out_enc,
    w_key_dec,
    w_value_dec,
    cotangent,
):
    return fused(
        owner_map * database.shape[0] + neighbour_ids,
        database,
        cond,
        norm_gain.reshape(1, -1),
        w_query_enc,
        w_out_enc,
        w_key_dec,
        w_value_dec,
        queries,
        cotangent,
    )


def solution(mesh):
    tokens = P(("seq", "enc"), None)
    return jax.shard_map(
        body,
        mesh=mesh,
        in_specs=(tokens, tokens, P("enc", None, None), tokens, tokens, P(), P(), P(), P(), P(), tokens),
        out_specs=(tokens,) * 7,
        check_vma=False,
    )
```

```python
import functools

import jax
import jax.numpy as jnp
from jax import lax
from jax.experimental import pallas as pl
from jax.experimental.pallas import tpu as pltpu
from jax.sharding import PartitionSpec as P

EPS = 1e-06
MESH = pl.DeviceIdType.MESH

F32, BF16 = jnp.float32, jnp.bfloat16
AXES = ("x", "y", "z")
TILES = 9
WHOLE_SLOTS = (
    (2, 3, 4, 5, 6, 7, 8, 9, 14),
    (5, 6, 7, 9, 11, 13, 14, 15, 17),
    (7, 8, 10, 12, 14, 16, 17, 18, 19),
    (10, 11, 13, 15, 17, 18, 19, 20, 21),
)
FIRST_AXES = (2, 0, 1, 2, 0, 2, 1, 2, 0)
HALF_SLOTS = ((15, 16), (17, 18), (19, 20), (21, 22))
SERVERS = ((0, 0), (0, 1), (1, 0), (1, -1), (2, 0), (2, 1), (3, 0), (3, -1))


def place():
    s, e = lax.axis_index("seq"), lax.axis_index("enc")
    return dict(core=s % 2, z=(s // 2) % 4, y=(s // 8) * 2 + e % 2, x=e // 2)


def device_of(at):
    y = at["y"]
    return ((y // 2) * 8 + at["z"] * 2 + at["core"], at["x"] * 2 + y % 2)


def moved(at, **steps):
    there = dict(at)
    for axis, step in steps.items():
        there[axis] = (at[axis] + step) % (2 if axis == "core" else 4)
    return there


def along(steps):
    p = (lax.axis_index("seq") * 8 + lax.axis_index("enc") + steps) % 128
    return (p // 8, p % 8)


def pick(index, values):
    if isinstance(index, int):
        return values[index]
    return jnp.where(index == 0, values[0], jnp.where(index == 1, values[1], values[2]))


def rows_of(axis, v):
    return ((0, 2 * v), (v // 2 * 4, v % 2), (v, 0))[axis]


def pick_pair(index, pairs):
    return tuple(pick(index, [pair[i] for pair in pairs]) for i in (0, 1))


class Map:
    def __init__(self):
        at = self.at = place()
        self.core = at["core"]
        self.other_core = device_of(moved(at, core=1))
        self.devices = [[device_of(moved(at, **{a: r})) for a in AXES] for r in range(4)]
        self.values = [[(at[a] + r) % 4 for a in AXES] for r in range(4)]
        self.places = [[rows_of(i, each[i]) for i in range(3)] for each in self.values]
        self.before, self.after = along(-1), along(1)


def remote(src, dst, send, recv, device):
    return pltpu.make_async_remote_copy(
        src_ref=src, dst_ref=dst, send_sem=send, recv_sem=recv, device_id=device, device_id_type=MESH
    )


def dot(a, b):
    return jnp.dot(a, b, preferred_element_type=F32)


def dot_nt(a, b):
    return lax.dot_general(a, b, (((1,), (1,)), ((), ())), preferred_element_type=F32)


def dot_tn(a, b):
    return lax.dot_general(a, b, (((0,), (0,)), ((), ())), preferred_element_type=F32)


class Tile:
    def __init__(self, map, t, turn, grads, came, sends, gets, kept, ssem, rsem, put):
        self.map, self.t, self.grads, self.came = map, t, grads, came
        self.sends, self.gets, self.kept = sends, gets, kept
        self.ssem, self.rsem, self.put = ssem, rsem, put
        if isinstance(turn, int):
            self.axes = [(turn + i) % 3 for i in range(3)]
        else:
            self.axes = [turn, jnp.where(turn == 2, 0, turn + 1), jnp.where(turn == 0, 2, turn - 1)]

    def value(self, level, r):
        return pick(self.axes[level], self.map.values[r])

    def copy(self, level, r=1):
        if level == 0:
            device, src, dst, sem = self.map.other_core, self.outgoing(), self.came, 0
        else:
            device = pick_pair(self.axes[level - 1], self.map.devices[r])
            src, dst, sem = self.sends[level - 1].at[r - 1], self.gets[level - 1].at[r - 1], 3 * level - 3 + r
        return remote(src, dst, self.ssem.at[self.t, sem], self.rsem.at[self.t, sem], device)

    def start(self):
        self.copy(0).start()

    def take(self, level):
        if level == 0:
            self.copy(0).wait_recv()
        else:
            for r in (1, 2, 3):
                self.copy(level, r).wait_recv()
        (self.take_core, self.take_first, self.take_second, self.take_third)[level]()

    def take_core(self):
        each = [
            [pick_pair(self.axes[level], [rows_of(a, v) for a in range(3)]) for v in range(4)] for level in (1, 2)
        ]
        rest = [tuple(a + b for a, b in zip(each[0][i // 4], each[1][i % 4])) for i in range(16)]
        for r in (2, 1, 3, 0):
            high, low = pick_pair(self.axes[0], self.map.places[r])
            for i in range(16):
                value = self.pair(high + rest[i][0], low + rest[i][1])
                if r:
                    self.sends[0][r - 1, i] = self.lower(value)
                else:
                    self.kept[0][i] = value
            if r:
                self.copy(1, r).start()
        self.copy(0).wait_send()

    def take_first(self):
        for r in (2, 1, 3, 0):
            first = self.value(1, r) * 4
            for i in range(4):
                c = first + i
                got = [self.higher(self.gets[0][q, c]) for q in range(3)]
                value = self.kept[0][c] + got[0] + got[1] + got[2]
                if r:
                    self.sends[1][r - 1, i] = value.astype(self.sends[1].dtype)
                else:
                    self.kept[1][i] = value
            if r:
                self.copy(2, r).start()

    def take_second(self):
        for r in (2, 1, 3, 0):
            c = self.value(2, r)
            got = [self.gets[1][q, c].astype(F32) for q in range(3)]
            value = self.kept[1][c] + got[0] + got[1] + got[2]
            if r:
                self.sends[2][r - 1, 0] = value.astype(self.sends[2].dtype)
                self.copy(3, r).start()
            else:
                self.kept[2][0] = value

    def take_third(self):
        got = [self.gets[2][q, 0].astype(F32) for q in range(3)]
        self.put(self.kept[2][0] + got[0] + got[1] + got[2])
        for level in (1, 2, 3):
            for r in (1, 2, 3):
                self.copy(level, r).wait_send()


class PairTile(Tile):
    def outgoing(self):
        return self.grads.at[:, :, 1 - self.map.core]

    def pair(self, high, low):
        core = self.map.core
        parts = [self.grads[i, high, core, low] + self.came[i, high, low] for i in (0, 1)]
        return jnp.concatenate(parts, axis=0)

    def lower(self, value):
        return value.astype(BF16)

    def higher(self, value):
        return value.astype(F32)


class HalfTile(Tile):
    def outgoing(self):
        return self.grads.at[:, 1 - self.map.core]

    def pair(self, high, low):
        return self.grads[high, self.map.core, low] + self.came[high, low]

    def lower(self, value):
        return jnp.concatenate([value[:, :128], value[:, 128:]], axis=0).astype(BF16)

    def higher(self, value):
        wide = value.astype(F32)
        return jnp.concatenate([wide[:8], wide[8:]], axis=1)


def by_head(x, reduce, neutral):
    low = lax.broadcasted_iota(jnp.int32, (x.shape[0], 128), 1) < 64
    parts = []
    for t in range(x.shape[1] // 128):
        one = x[:, t * 128 : t * 128 + 128]
        left = reduce(jnp.where(low, one, neutral), axis=-1, keepdims=True)
        right = reduce(jnp.where(low, neutral, one), axis=-1, keepdims=True)
        parts.append(jnp.where(low, left, right))
    return jnp.concatenate(parts, axis=1)


def head_blocks(x):
    wide = x.astype(F32)
    head = lax.broadcasted_iota(jnp.int32, x.shape, 1) // 64
    return jnp.concatenate([jnp.where(head == h, wide, 0.0) for h in range(4)], axis=0).astype(BF16)


def head_diagonal(x):
    head = lax.broadcasted_iota(jnp.int32, (64, 256), 1) // 64
    return sum(jnp.where(head == h, x[h * 64 : h * 64 + 64], 0.0) for h in range(4))


def two_heads(x):
    none = jnp.zeros((x.shape[0], 128), x.dtype)
    return jnp.concatenate(
        [jnp.concatenate([x[:, :128], none], axis=1), jnp.concatenate([none, x[:, 128:]], axis=1)], axis=0
    )


def own_heads(x):
    return jnp.concatenate([x[:64, :128], x[64:, 128:]], axis=1)


def main_kernel(
    codes, database, cond_in, gain, wq_in, wo_in, wk_in, wv_in, q_in, g_in,
    att, dq_out, dcond, gq_out, go_out, gk_out, gv_out,
    pool, cond, wq, wo, wk, wv, q_ref, g_ref,
    asked, asks, blocks_out, blocks, later,
    normed, query, probs, mixed, src, kv, dmix, last, first,
    grads, came, send1, get1, send2, get2, send3, get3, kept1, kept2, kept3,
    hcame, hsend1, hget1, hsend2, hget2, hsend3, hget3, hkept1, hkept2, hkept3,
    load_sem, ask_s, ask_r, block_s, block_r, ahead_s, ahead_r, shift_s, shift_r, ssem, rsem,
):
    map = Map()
    at = map.at
    me = lax.axis_index("seq") * 8 + lax.axis_index("enc")
    loads = [
        pltpu.make_async_copy(a, b, load_sem.at[i])
        for i, (a, b) in enumerate(
            (
                (database, pool), (cond_in, cond), (wq_in, wq), (wo_in, wo),
                (wk_in, wk), (wv_in, wv), (q_in, q_ref), (g_in, g_ref),
            )
        )
    ]
    loads[0].start()

    barrier = pltpu.get_barrier_semaphore()
    steps = {(dx * s % 4, dy * s % 4) for dx, dy in SERVERS for s in (1, -1)} | {(0, 2)}
    steps = sorted(steps - {(0, 0)})
    peers = [device_of(moved(at, x=dx, y=dy)) for dx, dy in steps]
    peers += [device_of(moved(at, core=1))] + [device_of(moved(at, z=r)) for r in (1, 2, 3)]
    peers += [map.before, map.after]
    for peer in peers:
        pl.semaphore_signal(barrier, inc=1, device_id=peer, device_id_type=MESH)
    pl.semaphore_wait(barrier, len(peers))

    first_row = [
        (((at["x"] + dx) % 4) * 2 + (at["y"] + dy) % 2) * 32 for dx, dy in SERVERS
    ]

    def served(code, r):
        return (code >= first_row[r]) & (code < first_row[r] + 32)

    def row_at(r):
        each = [codes[j, s] for s in range(3) for j in range(2)]
        return sum(jnp.where(served(code, r), code - first_row[r], 0) for code in each)

    asking, answers = [], []
    for r in (5, 7, 3, 4, 2, 6, 1):
        dx, dy = SERVERS[r]
        asks[r] = jnp.full((8, 128), row_at(r), jnp.int32)
        copy = remote(
            asks.at[r], asked.at[r], ask_s.at[r], ask_r.at[r], device_of(moved(at, x=dx, y=dy))
        )
        copy.start()
        asking.append((r, copy))
    for copy in loads[1:]:
        copy.start()
    loads[0].wait()
    for r, copy in asking:
        dx, dy = SERVERS[r]
        copy.wait_recv()
        blocks_out[r] = pool[jnp.max(asked[r])]
        answer = remote(
            blocks_out.at[r], blocks.at[r], block_s.at[r], block_r.at[r], device_of(moved(at, x=-dx, y=-dy))
        )
        answer.start()
        answers.append(answer)
    blocks[0] = pool[row_at(0)]
    for r, copy in asking:
        copy.wait_send()
    for copy in loads[1:4]:
        copy.wait()
    for answer in answers:
        answer.wait_recv()

    def encode(s, _):
        here = pl.ds(pl.multiple_of(s * 256, 256), 256)
        span = pl.ds(pl.multiple_of(s * 64, 64), 64)

        def wide():
            parts = []
            for j in range(2):
                code = codes[j, s]
                parts.append(blocks[sum(jnp.where(served(code, r), r, 0) for r in range(1, 8))])
            return jnp.concatenate(parts, axis=0).astype(F32)

        raw = wide()
        inverse = lax.rsqrt(jnp.mean(raw * raw, axis=-1, keepdims=True) + EPS)
        normed[here, :] = (raw * inverse * gain[...]).astype(BF16)
        query[here, :] = dot(normed[here, :], wq[...]).astype(BF16)
        cols = [slice(half * 256, half * 256 + 256) for half in range(2)]
        k4 = [head_blocks(cond[span, c]) for c in cols]
        v4 = [head_blocks(cond[span, 512 + half * 256 : 768 + half * 256]) for half in range(2)]
        scores = [dot_nt(query[here, cols[half]], k4[half]) * 0.125 for half in range(2)]
        e = [jnp.exp(x - by_head(x, jnp.max, -jnp.inf)) for x in scores]
        p = [x / by_head(x, jnp.sum, 0.0) for x in e]
        for half in range(2):
            probs[here, cols[half]] = p[half]
            mixed[here, cols[half]] = dot(p[half].astype(BF16), v4[half]).astype(BF16)
        src[here, :] = (wide() + dot(mixed[here, :], wo[...])).astype(BF16)
        return 0

    def ahead(t):
        cols = pl.ds(pl.multiple_of(t * 256, 256), 256)
        return [
            remote(
                ref.at[pl.ds(0, 64), cols], later.at[i, :, cols], ahead_s.at[i, t], ahead_r.at[i, t], map.before
            )
            for i, ref in enumerate((q_in, g_in))
        ]

    def send_ahead(t, _):
        for copy in ahead(t):
            copy.start()
        return 0

    lax.fori_loop(0, 8, send_ahead, 0)
    lax.fori_loop(0, 3, encode, 0)
    for copy in loads[4:]:
        copy.wait()
    for answer in answers:
        answer.wait_send()
    followed = jnp.where(me == 127, 0.0, 1.0).astype(BF16)

    def whole_tile(t):
        def put(total):
            def sheets():
                cols = pl.ds(pl.multiple_of(t * 256, 256), 256)
                gk_out[:, cols] = total[:8]
                gv_out[:, cols] = total[8:]

            def outer():
                for j in range(4):
                    go_out[:, j * 256 : j * 256 + 256] = total[j * 4 : j * 4 + 4]

            pl.when(t < 8)(sheets)
            pl.when(t == 8)(outer)

        turn = sum(jnp.where(t == i, a, 0) for i, a in enumerate(FIRST_AXES) if a)
        return PairTile(
            map, t, turn, grads.at[t % 3], came.at[t % 4],
            (send1.at[t], send2.at[t], send3.at[t]), (get1.at[t], get2.at[t], get3.at[t]),
            (kept1.at[t], kept2.at[t], kept3.at[t]), ssem, rsem, put,
        )

    def half_tile(i):
        def put(total):
            gq_out[:, pl.ds(pl.multiple_of(i * 256, 256), 256)] = total

        return HalfTile(
            map, TILES + i, 1 + i, grads.at[0, i], hcame.at[i],
            (hsend1.at[i], hsend2.at[i], hsend3.at[i]), (hget1.at[i], hget2.at[i], hget3.at[i]),
            (hkept1.at[i], hkept2.at[i], hkept3.at[i]), ssem, rsem, put,
        )

    scale = 128 ** (-0.5)

    def onward(t):
        cols = pl.ds(pl.multiple_of(t * 256, 256), 256)
        return [
            remote(last.at[i, :, cols], first.at[i, :, cols], shift_s.at[i, t], shift_r.at[i, t], map.after)
            for i in range(2)
        ]

    def half_rows(t):
        return t // 4 * 6, pl.ds(pl.multiple_of(t % 4 * 256, 256), 256)

    def decode(t):
        cols = pl.ds(pl.multiple_of(t * 256, 256), 256)
        base, pool_cols = half_rows(t)
        for copy in ahead(t):
            copy.wait()
        kv[0] = dot(src[...], wk[:, cols]).astype(BF16)
        kv[1] = dot(src[...], wv[:, cols]).astype(BF16)
        heres = [slice(s * 256, s * 256 + 256) for s in range(3)]
        afters = [slice(s * 64 + 64, s * 64 + 128) for s in range(3)]
        q2 = [two_heads(q_ref[a, cols]) for a in afters[:2]] + [two_heads(later[0, :, cols] * followed)]
        g2 = [two_heads(g_ref[a, cols]) for a in afters[:2]] + [two_heads(later[1, :, cols] * followed)]
        scores = [dot_nt(q2[s], kv[0, heres[s], :]) * scale for s in range(3)]
        dw = [dot_nt(g2[s], kv[1, heres[s], :]) for s in range(3)]
        e = [jnp.exp(x - jnp.max(x, axis=-1, keepdims=True)) for x in scores]
        p = [x / jnp.sum(x, axis=-1, keepdims=True) for x in e]
        w = [x.astype(BF16) for x in p]
        o = [own_heads(dot(w[s], kv[1, heres[s], :])).astype(BF16) for s in range(3)]
        dv = [dot_tn(w[s], g2[s]).astype(BF16) for s in range(3)]
        ds = [
            (p[s] * (dw[s] - jnp.sum(dw[s] * p[s], axis=-1, keepdims=True)) * scale).astype(BF16) for s in range(3)
        ]
        dq = [own_heads(dot(ds[s], kv[0, heres[s], :])).astype(BF16) for s in range(3)]
        dk = [dot_tn(ds[s], q2[s]).astype(BF16) for s in range(3)]
        for s in range(3):
            if s < 2:
                att[afters[s], cols] = o[s]
                dq_out[afters[s], cols] = dq[s]
            else:
                last[0, :, cols] = o[s]
                last[1, :, cols] = dq[s]
            low = base + s * 2
            pool[pl.ds(low, 2), :, pool_cols] = dk[s].reshape(2, 128, 256)
            pool[pl.ds(low + 12, 2), :, pool_cols] = dv[s].reshape(2, 128, 256)
        for i in range(2):
            sheet = dot_tn(src[...], pool[pl.ds(base + 12 * i, 6), :, pool_cols].reshape(768, 256))
            grads[t % 3, i] = sheet.reshape(8, 2, 8, 8, 256)
        for copy in onward(t):
            copy.start()

    def sources_back(i):
        cols = pl.ds(pl.multiple_of(i * 256, 256), 256)
        total = sum(
            dot_nt(pool[j * 6 : j * 6 + 6].reshape(768, 1024), w[cols, j % 2 * 1024 : j % 2 * 1024 + 1024])
            for j, w in enumerate((wk, wk, wv, wv))
        )
        pool[24:30, :, cols] = total.astype(BF16).reshape(6, 128, 256)

    def outer_out():
        for i in range(2):
            for j in range(2):
                cols = slice(i * 512 + j * 256, i * 512 + j * 256 + 256)
                sheet = dot_tn(mixed[...], pool[24:30, :, cols].reshape(768, 256))
                grads[1, j, 0:4] = sheet.reshape(4, 2, 8, 8, 256)

            def stack(g, _, i=i):
                for q in range(8):
                    left, right = (grads[1, j, g // 2, g % 2, q] for j in (0, 1))
                    for upper in range(2):
                        rows = slice(upper * 4, upper * 4 + 4)
                        p = 2 * q + upper
                        grads[2, i, g, p // 8, p % 8] = jnp.concatenate([left[rows], right[rows]], axis=0)
                return 0

            lax.fori_loop(0, 8, stack, 0)
        whole_tile(8).start()

    def mixed_back():
        dmix[...] = dot_nt(pool[24:30].reshape(768, 1024), wo[...]).astype(BF16)

    def query_back(half):
        cols = pl.ds(pl.multiple_of(half * 256, 256), 256)
        vcols = pl.ds(pl.multiple_of(half * 256 + 512, 256), 256)
        heres = [slice(s * 256, s * 256 + 256) for s in range(3)]
        spans = [slice(s * 64, s * 64 + 64) for s in range(3)]
        k4 = [head_blocks(cond[span, cols]) for span in spans]
        v4 = [head_blocks(cond[span, vcols]) for span in spans]
        dw = [dot_nt(dmix[heres[s], cols], v4[s]) for s in range(3)]
        p = [probs[here, cols] for here in heres]
        sums = [by_head(dw[s] * p[s], jnp.sum, 0.0) for s in range(3)]
        ds = [(p[s] * (dw[s] - sums[s]) * 0.125).astype(BF16) for s in range(3)]
        for s in range(3):
            mixed[heres[s], cols] = ds[s]
            kv[half, heres[s], :] = dot(ds[s], k4[s]).astype(BF16)
        grads[0, half] = dot_tn(normed[...], kv[half]).reshape(8, 2, 8, 8, 256)
        half_tile(half).start()

    def cond_back():
        def some(i, _):
            s, half = i // 2, i % 2
            here = pl.ds(pl.multiple_of(s * 256, 256), 256)
            span = pl.ds(pl.multiple_of(s * 64, 64), 64)
            cols = pl.ds(pl.multiple_of(half * 256, 256), 256)
            vcols = pl.ds(pl.multiple_of(half * 256 + 512, 256), 256)
            w = probs[here, cols].astype(BF16)
            dcond[span, vcols] = head_diagonal(dot_tn(w, dmix[here, cols])).astype(BF16)
            dcond[span, cols] = head_diagonal(dot_tn(mixed[here, cols], query[here, cols])).astype(BF16)
            return 0

        lax.fori_loop(0, 6, some, 0)

    def tile_at(slot, slots):
        return sum(jnp.where(slot == at_slot, t + 1, 0) for t, at_slot in enumerate(slots)) - 1

    def step(slot, _):
        pl.when(slot < 8)(lambda: decode(slot))
        pl.when((slot >= 8) & (slot < 12))(lambda: sources_back(slot - 8))
        pl.when(slot == 12)(outer_out)
        pl.when(slot == 13)(mixed_back)
        pl.when((slot == 14) | (slot == 15))(lambda: query_back(slot - 14))
        pl.when(slot == 16)(cond_back)
        for level in (3, 2, 1, 0):
            t = tile_at(slot, WHOLE_SLOTS[level])
            pl.when(t >= 0)(lambda t=t, level=level: whole_tile(t).take(level))
        pl.when(slot < 8)(lambda: whole_tile(slot).start())
        for level in (3, 2, 1, 0):
            i = tile_at(slot, HALF_SLOTS[level])
            pl.when(i >= 0)(lambda i=i, level=level: half_tile(i).take(level))
        return 0

    lax.fori_loop(0, 23, step, 0)

    def arrive(t, _):
        for copy in onward(t):
            copy.wait()
        return 0

    lax.fori_loop(0, 8, arrive, 0)
    followed_by = jnp.where(me == 0, 0.0, 1.0).astype(BF16)
    att[:64, :] = first[0] * followed_by
    dq_out[:64, :] = first[1] * followed_by


def fused(codes, database, cond, gain, wq, wo, wk, wv, queries, grads):
    vmem, smem = pl.BlockSpec(memory_space=pltpu.VMEM), pl.BlockSpec(memory_space=pltpu.SMEM)
    hbm = pl.BlockSpec(memory_space=pl.ANY)
    shape, dma = jax.ShapeDtypeStruct, pltpu.SemaphoreType.DMA
    half = lambda *dims: pltpu.VMEM(dims, BF16)
    full = lambda *dims: pltpu.VMEM(dims, F32)
    outs = pl.pallas_call(
        main_kernel,
        out_shape=(
            shape((192, 2048), BF16),
            shape((192, 2048), BF16),
            shape((192, 1024), BF16),
            shape((8, 512), F32),
            shape((4, 1024), F32),
            shape((8, 2048), F32),
            shape((8, 2048), F32),
        ),
        in_specs=[smem, hbm, hbm, vmem] + [hbm] * 6,
        out_specs=(vmem,) * 7,
        scratch_shapes=[
            half(32, 128, 1024), half(192, 1024), half(1024, 512), half(512, 1024),
            half(1024, 2048), half(1024, 2048), half(192, 2048), half(192, 2048),
            pltpu.VMEM((8, 8, 128), jnp.int32), pltpu.VMEM((8, 8, 128), jnp.int32),
            half(8, 128, 1024), half(8, 128, 1024), half(2, 64, 2048),
            half(768, 1024), half(768, 512), full(768, 512), half(768, 512), half(768, 1024),
            half(2, 768, 256), half(768, 512),
            half(2, 64, 2048), half(2, 64, 2048),
            full(3, 2, 8, 2, 8, 8, 256), full(4, 2, 8, 8, 8, 256),
            half(TILES, 3, 16, 16, 256), half(TILES, 3, 16, 16, 256),
            half(TILES, 3, 4, 16, 256), half(TILES, 3, 4, 16, 256),
            half(TILES, 3, 1, 16, 256), half(TILES, 3, 1, 16, 256),
            full(TILES, 16, 16, 256), full(TILES, 4, 16, 256), full(TILES, 1, 16, 256),
            full(2, 8, 8, 8, 256), half(2, 3, 16, 16, 128), half(2, 3, 16, 16, 128),
            full(2, 3, 4, 8, 256), full(2, 3, 4, 8, 256), full(2, 3, 1, 8, 256), full(2, 3, 1, 8, 256),
            full(2, 16, 8, 256), full(2, 4, 8, 256), full(2, 1, 8, 256),
            dma((8,)), dma((8,)), dma((8,)), dma((8,)), dma((8,)), dma((2, 8)), dma((2, 8)), dma((2, 8)), dma((2, 8)),
            dma((TILES + 2, 10)), dma((TILES + 2, 10)),
        ],
        compiler_params=pltpu.CompilerParams(
            collective_id=0, has_side_effects=True, vmem_limit_bytes=63 * 1024 * 1024
        ),
    )(codes, database, cond, gain, wq, wo, wk, wv, queries, grads)

    def leave(*refs):
        n, sem = len(outs), refs[-1]
        copies = [pltpu.make_async_copy(refs[i], refs[n + i], sem.at[i]) for i in range(n)]
        for copy in copies:
            copy.start()
        for copy in copies:
            copy.wait()

    return pl.pallas_call(
        leave,
        out_shape=tuple(shape(o.shape, o.dtype) for o in outs),
        in_specs=[hbm] * len(outs),
        out_specs=(vmem,) * len(outs),
        scratch_shapes=[dma((len(outs),))],
    )(*outs)


def body(
    queries,
    cond,
    database,
    neighbour_ids,
    owner_map,
    norm_gain,
    w_query_enc,
    w_out_enc,
    w_key_dec,
    w_value_dec,
    cotangent,
):
    return fused(
        owner_map.T * database.shape[0] + neighbour_ids.T,
        database,
        cond,
        norm_gain.reshape(1, -1),
        w_query_enc,
        w_out_enc,
        w_key_dec,
        w_value_dec,
        queries,
        cotangent,
    )


def solution(mesh):
    tokens = P(("seq", "enc"), None)
    return jax.shard_map(
        body,
        mesh=mesh,
        in_specs=(tokens, tokens, P("enc", None, None), tokens, tokens, P(), P(), P(), P(), P(), tokens),
        out_specs=(tokens,) * 7,
        check_vma=False,
    )
```

```python
import functools

import jax
import jax.numpy as jnp
from jax import lax
from jax.experimental import pallas as pl
from jax.experimental.pallas import tpu as pltpu
from jax.sharding import PartitionSpec as P

EPS = 1e-06
MESH = pl.DeviceIdType.MESH

F32, BF16 = jnp.float32, jnp.bfloat16
AXES = ("x", "y", "z")
TILES = 9
WHOLE_SLOTS = (
    (2, 3, 4, 5, 6, 7, 8, 9, 14),
    (6, 7, 8, 10, 11, 13, 15, 16, 18),
    (8, 9, 11, 13, 14, 16, 17, 18, 20),
    (10, 12, 14, 16, 17, 18, 19, 21, 22),
)
HALF_SLOTS = ((15, 16), (17, 18), (19, 20), (21, 22))
STEPS = 23
FIRST_AXES = (2, 0, 1, 2, 0, 2, 1, 2, 0)
HALF_SLOTS = ((15, 16), (17, 18), (19, 20), (21, 22))
SERVERS = ((0, 0), (0, 1), (1, 0), (1, -1), (2, 0), (2, 1), (3, 0), (3, -1))


def place():
    s, e = lax.axis_index("seq"), lax.axis_index("enc")
    return dict(core=s % 2, z=(s // 2) % 4, y=(s // 8) * 2 + e % 2, x=e // 2)


def device_of(at):
    y = at["y"]
    return ((y // 2) * 8 + at["z"] * 2 + at["core"], at["x"] * 2 + y % 2)


def moved(at, **steps):
    there = dict(at)
    for axis, step in steps.items():
        there[axis] = (at[axis] + step) % (2 if axis == "core" else 4)
    return there


def along(steps):
    p = (lax.axis_index("seq") * 8 + lax.axis_index("enc") + steps) % 128
    return (p // 8, p % 8)


def pick(index, values):
    if isinstance(index, int):
        return values[index]
    return jnp.where(index == 0, values[0], jnp.where(index == 1, values[1], values[2]))


def rows_of(axis, v):
    return ((0, 2 * v), (v // 2 * 4, v % 2), (v, 0))[axis]


def pick_pair(index, pairs):
    return tuple(pick(index, [pair[i] for pair in pairs]) for i in (0, 1))


class Map:
    def __init__(self):
        at = self.at = place()
        self.core = at["core"]
        self.other_core = device_of(moved(at, core=1))
        self.devices = [[device_of(moved(at, **{a: r})) for a in AXES] for r in range(4)]
        self.values = [[(at[a] + r) % 4 for a in AXES] for r in range(4)]
        self.places = [[rows_of(i, each[i]) for i in range(3)] for each in self.values]
        self.before, self.after = along(-1), along(1)


def remote(src, dst, send, recv, device):
    return pltpu.make_async_remote_copy(
        src_ref=src, dst_ref=dst, send_sem=send, recv_sem=recv, device_id=device, device_id_type=MESH
    )


def dot(a, b):
    return jnp.dot(a, b, preferred_element_type=F32)


def dot_nt(a, b):
    return lax.dot_general(a, b, (((1,), (1,)), ((), ())), preferred_element_type=F32)


def dot_tn(a, b):
    return lax.dot_general(a, b, (((0,), (0,)), ((), ())), preferred_element_type=F32)


class Tile:
    def __init__(self, map, t, turn, grads, came, sends, gets, kept, ssem, rsem, put):
        self.map, self.t, self.grads, self.came = map, t, grads, came
        self.sends, self.gets, self.kept = sends, gets, kept
        self.ssem, self.rsem, self.put = ssem, rsem, put
        if isinstance(turn, int):
            self.axes = [(turn + i) % 3 for i in range(3)]
        else:
            self.axes = [turn, jnp.where(turn == 2, 0, turn + 1), jnp.where(turn == 0, 2, turn - 1)]

    def value(self, level, r):
        return pick(self.axes[level], self.map.values[r])

    def copy(self, level, r=1):
        if level == 0:
            device, src, dst, sem = self.map.other_core, self.outgoing(), self.came, 0
        else:
            device = pick_pair(self.axes[level - 1], self.map.devices[r])
            src, dst, sem = self.sends[level - 1].at[r - 1], self.gets[level - 1].at[r - 1], 3 * level - 3 + r
        return remote(src, dst, self.ssem.at[self.t, sem], self.rsem.at[self.t, sem], device)

    def start(self):
        self.copy(0).start()

    def take(self, level):
        if level == 0:
            self.copy(0).wait_recv()
        else:
            for r in (1, 2, 3):
                self.copy(level, r).wait_recv()
        (self.take_core, self.take_first, self.take_second, self.take_third)[level]()

    def take_core(self):
        each = [
            [pick_pair(self.axes[level], [rows_of(a, v) for a in range(3)]) for v in range(4)] for level in (1, 2)
        ]
        rest = [tuple(a + b for a, b in zip(each[0][i // 4], each[1][i % 4])) for i in range(16)]
        for r in (2, 1, 3, 0):
            high, low = pick_pair(self.axes[0], self.map.places[r])
            for i in range(16):
                value = self.pair(high + rest[i][0], low + rest[i][1])
                if r:
                    self.sends[0][r - 1, i] = self.lower(value)
                else:
                    self.kept[0][i] = value
            if r:
                self.copy(1, r).start()
        self.copy(0).wait_send()

    def take_first(self):
        for r in (2, 1, 3, 0):
            first = self.value(1, r) * 4
            for i in range(4):
                c = first + i
                got = [self.higher(self.gets[0][q, c]) for q in range(3)]
                value = self.kept[0][c] + got[0] + got[1] + got[2]
                if r:
                    self.sends[1][r - 1, i] = value.astype(self.sends[1].dtype)
                else:
                    self.kept[1][i] = value
            if r:
                self.copy(2, r).start()

    def take_second(self):
        for r in (2, 1, 3, 0):
            c = self.value(2, r)
            got = [self.gets[1][q, c].astype(F32) for q in range(3)]
            value = self.kept[1][c] + got[0] + got[1] + got[2]
            if r:
                self.sends[2][r - 1, 0] = value.astype(self.sends[2].dtype)
                self.copy(3, r).start()
            else:
                self.kept[2][0] = value

    def take_third(self):
        got = [self.gets[2][q, 0].astype(F32) for q in range(3)]
        self.put(self.kept[2][0] + got[0] + got[1] + got[2])
        for level in (1, 2, 3):
            for r in (1, 2, 3):
                self.copy(level, r).wait_send()


class PairTile(Tile):
    def outgoing(self):
        return self.grads.at[:, :, 1 - self.map.core]

    def pair(self, high, low):
        core = self.map.core
        parts = [self.grads[i, high, core, low] + self.came[i, high, low] for i in (0, 1)]
        return jnp.concatenate(parts, axis=0)

    def lower(self, value):
        return value.astype(BF16)

    def higher(self, value):
        return value.astype(F32)


class HalfTile(Tile):
    def outgoing(self):
        return self.grads.at[:, 1 - self.map.core]

    def pair(self, high, low):
        return self.grads[high, self.map.core, low] + self.came[high, low]

    def lower(self, value):
        return jnp.concatenate([value[:, :128], value[:, 128:]], axis=0).astype(BF16)

    def higher(self, value):
        wide = value.astype(F32)
        return jnp.concatenate([wide[:8], wide[8:]], axis=1)


def by_head(x, reduce, neutral):
    low = lax.broadcasted_iota(jnp.int32, (x.shape[0], 128), 1) < 64
    parts = []
    for t in range(x.shape[1] // 128):
        one = x[:, t * 128 : t * 128 + 128]
        left = reduce(jnp.where(low, one, neutral), axis=-1, keepdims=True)
        right = reduce(jnp.where(low, neutral, one), axis=-1, keepdims=True)
        parts.append(jnp.where(low, left, right))
    return jnp.concatenate(parts, axis=1)


def head_blocks(x):
    wide = x.astype(F32)
    head = lax.broadcasted_iota(jnp.int32, x.shape, 1) // 64
    return jnp.concatenate([jnp.where(head == h, wide, 0.0) for h in range(4)], axis=0).astype(BF16)


def head_diagonal(x):
    head = lax.broadcasted_iota(jnp.int32, (64, 256), 1) // 64
    return sum(jnp.where(head == h, x[h * 64 : h * 64 + 64], 0.0) for h in range(4))


def two_heads(x):
    none = jnp.zeros((x.shape[0], 128), x.dtype)
    return jnp.concatenate(
        [jnp.concatenate([x[:, :128], none], axis=1), jnp.concatenate([none, x[:, 128:]], axis=1)], axis=0
    )


def own_heads(x):
    return jnp.concatenate([x[:64, :128], x[64:, 128:]], axis=1)


def main_kernel(
    ids, owners, database, cond_in, gain, wq_in, wo_in, wk_in, wv_in, q_in, g_in,
    att, dq_out, dcond, gq_out, go_out, gk_out, gv_out,
    pool, cond, wq, wo, wk, wv, q_ref, g_ref,
    asked, asks, blocks_out, upper_rows, lower_rows, later,
    normed, query, probs, mixed, src, kv, dmix, last, first,
    grads, came, send1, get1, send2, get2, send3, get3, kept1, kept2, kept3,
    hcame, hsend1, hget1, hsend2, hget2, hsend3, hget3, hkept1, hkept2, hkept3,
    load_sem, ask_s, ask_r, block_s, block_r, ahead_s, ahead_r, shift_s, shift_r, ssem, rsem,
):
    map = Map()
    at = map.at
    me = lax.axis_index("seq") * 8 + lax.axis_index("enc")
    loads = [
        pltpu.make_async_copy(a, b, load_sem.at[i])
        for i, (a, b) in enumerate(
            (
                (database, pool), (cond_in, cond), (wq_in, wq), (wo_in, wo),
                (wk_in, wk), (wv_in, wv), (q_in, q_ref), (g_in, g_ref),
            )
        )
    ]
    loads[0].start()

    barrier = pltpu.get_barrier_semaphore()
    steps = {(dx * s % 4, dy * s % 4) for dx, dy in SERVERS for s in (1, -1)} | {(0, 2)}
    steps = sorted(steps - {(0, 0)})
    peers = [device_of(moved(at, x=dx, y=dy)) for dx, dy in steps]
    peers += [device_of(moved(at, core=1))] + [device_of(moved(at, z=r)) for r in (1, 2, 3)]
    peers += [map.before, map.after]
    for peer in peers:
        pl.semaphore_signal(barrier, inc=1, device_id=peer, device_id_type=MESH)
    pl.semaphore_wait(barrier, len(peers))

    server = [((at["x"] + dx) % 4) * 2 + (at["y"] + dy) % 2 for dx, dy in SERVERS]

    def row_at(r):
        each = [(owners[j, s], ids[j, s]) for s in range(3) for j in range(2)]
        return sum(jnp.where(owner == server[r], row, 0) for owner, row in each)

    asking, answers = [], []
    for r in (5, 7, 3, 4, 2, 6, 1):
        dx, dy = SERVERS[r]
        asks[r] = jnp.full((8, 128), row_at(r), jnp.int32)
        copy = remote(
            asks.at[r], asked.at[r], ask_s.at[r], ask_r.at[r], device_of(moved(at, x=dx, y=dy))
        )
        copy.start()
        asking.append((r, copy))
    for copy in loads[1:]:
        copy.start()
    loads[0].wait()
    blocks = (upper_rows, lower_rows)
    for h in range(2):
        part = pl.ds(h * 64, 64)
        for r, copy in asking:
            dx, dy = SERVERS[r]
            if h == 0:
                copy.wait_recv()
                blocks_out[r] = pool[jnp.max(asked[r])]
            answer = remote(
                blocks_out.at[r, part], blocks[h].at[r], block_s.at[h, r], block_r.at[h, r],
                device_of(moved(at, x=-dx, y=-dy)),
            )
            answer.start()
            answers.append(answer)
    own = pool[row_at(0)]
    for h in range(2):
        blocks[h][0] = own[h * 64 : h * 64 + 64]
    for r, copy in asking:
        copy.wait_send()
    for copy in loads[1:4]:
        copy.wait()
    slots = [
        [sum(jnp.where(owners[j, s] == server[r], r, 0) for r in range(1, 8)) for j in range(2)] for s in range(3)
    ]

    def encode(h):
        low = h * 384
        both = slice(low, low + 384)
        for s in range(3):
            for j in range(2):
                at_rows = slice(low + s * 128 + j * 64, low + s * 128 + j * 64 + 64)
                raw = blocks[h][slots[s][j]].astype(F32)
                inverse = lax.rsqrt(jnp.mean(raw * raw, axis=-1, keepdims=True) + EPS)
                normed[at_rows, :] = (raw * inverse * gain[...]).astype(BF16)
        query[both, :] = dot(normed[both, :], wq[...]).astype(BF16)
        pieces = [(s, slice(c * 256, c * 256 + 256)) for s in range(3) for c in range(2)]
        here = [slice(low + s * 128, low + s * 128 + 128) for s in range(3)]
        span = [slice(s * 64, s * 64 + 64) for s in range(3)]
        k4 = [head_blocks(cond[span[s], c]) for s, c in pieces]
        v4 = [head_blocks(cond[span[s], c.start + 512 : c.stop + 512]) for s, c in pieces]
        scores = [dot_nt(query[here[s], c], k) * 0.125 for (s, c), k in zip(pieces, k4)]
        e = [jnp.exp(x - by_head(x, jnp.max, -jnp.inf)) for x in scores]
        p = [x / by_head(x, jnp.sum, 0.0) for x in e]
        for (s, c), x, v in zip(pieces, p, v4):
            probs[here[s], c] = x
            mixed[here[s], c] = dot(x.astype(BF16), v).astype(BF16)
        out = dot(mixed[both, :], wo[...])
        for s in range(3):
            for j in range(2):
                i = s * 128 + j * 64
                raw = blocks[h][slots[s][j]].astype(F32)
                src[low + i : low + i + 64, :] = (raw + out[i : i + 64]).astype(BF16)

    for answer in answers[:7]:
        answer.wait_recv()
    encode(0)
    for answer in answers[7:]:
        answer.wait_recv()

    def ahead(t):
        cols = pl.ds(pl.multiple_of(t * 256, 256), 256)
        return [
            remote(
                ref.at[pl.ds(0, 64), cols], later.at[i, :, cols], ahead_s.at[i, t], ahead_r.at[i, t], map.before
            )
            for i, ref in enumerate((q_in, g_in))
        ]

    def send_ahead(t, _):
        for copy in ahead(t):
            copy.start()
        return 0

    lax.fori_loop(0, 8, send_ahead, 0)
    encode(1)
    for copy in loads[4:]:
        copy.wait()
    for answer in answers:
        answer.wait_send()
    followed = jnp.where(me == 127, 0.0, 1.0).astype(BF16)

    def whole_tile(t):
        def put(total):
            def sheets():
                cols = pl.ds(pl.multiple_of(t * 256, 256), 256)
                gk_out[:, cols] = total[:8]
                gv_out[:, cols] = total[8:]

            def outer():
                for j in range(4):
                    go_out[:, j * 256 : j * 256 + 256] = total[j * 4 : j * 4 + 4]

            pl.when(t < 8)(sheets)
            pl.when(t == 8)(outer)

        turn = sum(jnp.where(t == i, a, 0) for i, a in enumerate(FIRST_AXES) if a)
        return PairTile(
            map, t, turn, grads.at[t % 3], came.at[t % 4],
            (send1.at[t], send2.at[t], send3.at[t]), (get1.at[t], get2.at[t], get3.at[t]),
            (kept1.at[t], kept2.at[t], kept3.at[t]), ssem, rsem, put,
        )

    def half_tile(i):
        def put(total):
            gq_out[:, pl.ds(pl.multiple_of(i * 256, 256), 256)] = total

        return HalfTile(
            map, TILES + i, 1 + i, grads.at[0, i], hcame.at[i],
            (hsend1.at[i], hsend2.at[i], hsend3.at[i]), (hget1.at[i], hget2.at[i], hget3.at[i]),
            (hkept1.at[i], hkept2.at[i], hkept3.at[i]), ssem, rsem, put,
        )

    scale = 128 ** (-0.5)

    def onward(t):
        cols = pl.ds(pl.multiple_of(t * 256, 256), 256)
        return [
            remote(last.at[i, :, cols], first.at[i, :, cols], shift_s.at[i, t], shift_r.at[i, t], map.after)
            for i in range(2)
        ]

    def of_span(ref, s, cols):
        return jnp.concatenate([ref[h * 384 + s * 128 : h * 384 + s * 128 + 128, cols] for h in range(2)], axis=0)

    def half_rows(t):
        return t // 4 * 6, pl.ds(pl.multiple_of(t % 4 * 256, 256), 256)

    def decode(t):
        cols = pl.ds(pl.multiple_of(t * 256, 256), 256)
        base, pool_cols = half_rows(t)
        for copy in ahead(t):
            copy.wait()
        kv[0] = dot(src[...], wk[:, cols]).astype(BF16)
        kv[1] = dot(src[...], wv[:, cols]).astype(BF16)
        k, v = ([of_span(kv.at[i], s, slice(None)) for s in range(3)] for i in range(2))
        afters = [slice(s * 64 + 64, s * 64 + 128) for s in range(3)]
        q2 = [two_heads(q_ref[a, cols]) for a in afters[:2]] + [two_heads(later[0, :, cols] * followed)]
        g2 = [two_heads(g_ref[a, cols]) for a in afters[:2]] + [two_heads(later[1, :, cols] * followed)]
        scores = [dot_nt(q2[s], k[s]) * scale for s in range(3)]
        dw = [dot_nt(g2[s], v[s]) for s in range(3)]
        e = [jnp.exp(x - jnp.max(x, axis=-1, keepdims=True)) for x in scores]
        p = [x / jnp.sum(x, axis=-1, keepdims=True) for x in e]
        w = [x.astype(BF16) for x in p]
        o = [own_heads(dot(w[s], v[s])).astype(BF16) for s in range(3)]
        dv = [dot_tn(w[s], g2[s]).astype(BF16) for s in range(3)]
        ds = [
            (p[s] * (dw[s] - jnp.sum(dw[s] * p[s], axis=-1, keepdims=True)) * scale).astype(BF16) for s in range(3)
        ]
        dq = [own_heads(dot(ds[s], k[s])).astype(BF16) for s in range(3)]
        dk = [dot_tn(ds[s], q2[s]).astype(BF16) for s in range(3)]
        for s in range(3):
            if s < 2:
                att[afters[s], cols] = o[s]
                dq_out[afters[s], cols] = dq[s]
            else:
                last[0, :, cols] = o[s]
                last[1, :, cols] = dq[s]
            for h in range(2):
                pool[base + h * 3 + s, :, pool_cols] = dk[s][h * 128 : h * 128 + 128]
                pool[base + h * 3 + s + 12, :, pool_cols] = dv[s][h * 128 : h * 128 + 128]
        for i in range(2):
            sheet = dot_tn(src[...], pool[pl.ds(base + 12 * i, 6), :, pool_cols].reshape(768, 256))
            grads[t % 3, i] = sheet.reshape(8, 2, 8, 8, 256)
        for copy in onward(t):
            copy.start()

    def sources_back(i):
        cols = pl.ds(pl.multiple_of(i * 256, 256), 256)
        total = sum(
            dot_nt(pool[j * 6 : j * 6 + 6].reshape(768, 1024), w[cols, j % 2 * 1024 : j % 2 * 1024 + 1024])
            for j, w in enumerate((wk, wk, wv, wv))
        )
        pool[24:30, :, cols] = total.astype(BF16).reshape(6, 128, 256)

    def outer_out():
        for i in range(2):
            for j in range(2):
                cols = slice(i * 512 + j * 256, i * 512 + j * 256 + 256)
                sheet = dot_tn(mixed[...], pool[24:30, :, cols].reshape(768, 256))
                grads[1, j, 0:4] = sheet.reshape(4, 2, 8, 8, 256)

            def stack(g, _, i=i):
                for q in range(8):
                    left, right = (grads[1, j, g // 2, g % 2, q] for j in (0, 1))
                    for upper in range(2):
                        rows = slice(upper * 4, upper * 4 + 4)
                        p = 2 * q + upper
                        grads[2, i, g, p // 8, p % 8] = jnp.concatenate([left[rows], right[rows]], axis=0)
                return 0

            lax.fori_loop(0, 8, stack, 0)
        whole_tile(8).start()

    def mixed_back():
        dmix[...] = dot_nt(pool[24:30].reshape(768, 1024), wo[...]).astype(BF16)

    def query_back(half):
        cols = pl.ds(pl.multiple_of(half * 256, 256), 256)
        vcols = pl.ds(pl.multiple_of(half * 256 + 512, 256), 256)
        spans = [slice(s * 64, s * 64 + 64) for s in range(3)]
        k4 = [head_blocks(cond[span, cols]) for span in spans]
        v4 = [head_blocks(cond[span, vcols]) for span in spans]
        dw = [dot_nt(of_span(dmix, s, cols), v4[s]) for s in range(3)]
        p = [of_span(probs, s, cols) for s in range(3)]
        sums = [by_head(dw[s] * p[s], jnp.sum, 0.0) for s in range(3)]
        ds = [(p[s] * (dw[s] - sums[s]) * 0.125).astype(BF16) for s in range(3)]
        for s in range(3):
            dquery = dot(ds[s], k4[s]).astype(BF16)
            for h in range(2):
                rows, part = pl.ds(h * 384 + s * 128, 128), slice(h * 128, h * 128 + 128)
                mixed[rows, cols] = ds[s][part]
                kv[half, rows, :] = dquery[part]
        grads[0, half] = dot_tn(normed[...], kv[half]).reshape(8, 2, 8, 8, 256)
        half_tile(half).start()

    def cond_back():
        def some(i, _):
            s, half = i // 2, i % 2
            span = pl.ds(pl.multiple_of(s * 64, 64), 64)
            cols = pl.ds(pl.multiple_of(half * 256, 256), 256)
            vcols = pl.ds(pl.multiple_of(half * 256 + 512, 256), 256)

            def both(ref):
                parts = [ref[pl.ds(pl.multiple_of(h * 384 + s * 128, 128), 128), cols] for h in range(2)]
                return jnp.concatenate(parts, axis=0)

            w = both(probs).astype(BF16)
            dcond[span, vcols] = head_diagonal(dot_tn(w, both(dmix))).astype(BF16)
            dcond[span, cols] = head_diagonal(dot_tn(both(mixed), both(query))).astype(BF16)
            return 0

        lax.fori_loop(0, 6, some, 0)

    def tile_at(slot, slots):
        return sum(jnp.where(slot == at_slot, t + 1, 0) for t, at_slot in enumerate(slots)) - 1

    def step(slot, _):
        pl.when(slot < 8)(lambda: decode(slot))
        pl.when((slot >= 8) & (slot < 12))(lambda: sources_back(slot - 8))
        pl.when(slot == 12)(outer_out)
        pl.when(slot == 13)(mixed_back)
        pl.when((slot == 14) | (slot == 15))(lambda: query_back(slot - 14))
        pl.when(slot == 16)(cond_back)
        def take_halves(levels):
            for level in levels:
                i = tile_at(slot, HALF_SLOTS[level])
                pl.when(i >= 0)(lambda i=i, level=level: half_tile(i).take(level))

        take_halves((3, 2, 1))
        for level in (3, 2, 1, 0):
            t = tile_at(slot, WHOLE_SLOTS[level])
            pl.when(t >= 0)(lambda t=t, level=level: whole_tile(t).take(level))
        take_halves((0,))
        pl.when(slot < 8)(lambda: whole_tile(slot).start())
        return 0

    lax.fori_loop(0, STEPS, step, 0)

    def arrive(t, _):
        for copy in onward(t):
            copy.wait()
        return 0

    lax.fori_loop(0, 8, arrive, 0)
    followed_by = jnp.where(me == 0, 0.0, 1.0).astype(BF16)
    att[:64, :] = first[0] * followed_by
    dq_out[:64, :] = first[1] * followed_by


def fused(ids, owners, database, cond, gain, wq, wo, wk, wv, queries, grads):
    vmem, smem = pl.BlockSpec(memory_space=pltpu.VMEM), pl.BlockSpec(memory_space=pltpu.SMEM)
    hbm = pl.BlockSpec(memory_space=pl.ANY)
    shape, dma = jax.ShapeDtypeStruct, pltpu.SemaphoreType.DMA
    half = lambda *dims: pltpu.VMEM(dims, BF16)
    full = lambda *dims: pltpu.VMEM(dims, F32)
    outs = pl.pallas_call(
        main_kernel,
        out_shape=(
            shape((192, 2048), BF16),
            shape((192, 2048), BF16),
            shape((192, 1024), BF16),
            shape((8, 512), F32),
            shape((4, 1024), F32),
            shape((8, 2048), F32),
            shape((8, 2048), F32),
        ),
        in_specs=[smem, smem, hbm, hbm, vmem] + [hbm] * 6,
        out_specs=(vmem,) * 7,
        scratch_shapes=[
            half(32, 128, 1024), half(192, 1024), half(1024, 512), half(512, 1024),
            half(1024, 2048), half(1024, 2048), half(192, 2048), half(192, 2048),
            pltpu.VMEM((8, 8, 128), jnp.int32), pltpu.VMEM((8, 8, 128), jnp.int32),
            half(8, 128, 1024), half(8, 64, 1024), half(8, 64, 1024), half(2, 64, 2048),
            half(768, 1024), half(768, 512), full(768, 512), half(768, 512), half(768, 1024),
            half(2, 768, 256), half(768, 512),
            half(2, 64, 2048), half(2, 64, 2048),
            full(3, 2, 8, 2, 8, 8, 256), full(4, 2, 8, 8, 8, 256),
            half(TILES, 3, 16, 16, 256), half(TILES, 3, 16, 16, 256),
            half(TILES, 3, 4, 16, 256), half(TILES, 3, 4, 16, 256),
            half(TILES, 3, 1, 16, 256), half(TILES, 3, 1, 16, 256),
            full(TILES, 16, 16, 256), full(TILES, 4, 16, 256), full(TILES, 1, 16, 256),
            full(2, 8, 8, 8, 256), half(2, 3, 16, 16, 128), half(2, 3, 16, 16, 128),
            full(2, 3, 4, 8, 256), full(2, 3, 4, 8, 256), full(2, 3, 1, 8, 256), full(2, 3, 1, 8, 256),
            full(2, 16, 8, 256), full(2, 4, 8, 256), full(2, 1, 8, 256),
            dma((8,)), dma((8,)), dma((8,)), dma((2, 8)), dma((2, 8)), dma((2, 8)), dma((2, 8)), dma((2, 8)), dma((2, 8)),
            dma((TILES + 2, 10)), dma((TILES + 2, 10)),
        ],
        compiler_params=pltpu.CompilerParams(
            collective_id=0, has_side_effects=True, vmem_limit_bytes=63 * 1024 * 1024
        ),
    )(ids, owners, database, cond, gain, wq, wo, wk, wv, queries, grads)

    def leave(*refs):
        n, sem = len(outs), refs[-1]
        copies = [pltpu.make_async_copy(refs[i], refs[n + i], sem.at[i]) for i in range(n)]
        for copy in copies:
            copy.start()
        for copy in copies:
            copy.wait()

    return pl.pallas_call(
        leave,
        out_shape=tuple(shape(o.shape, o.dtype) for o in outs),
        in_specs=[hbm] * len(outs),
        out_specs=(vmem,) * len(outs),
        scratch_shapes=[dma((len(outs),))],
    )(*outs)


def body(
    queries,
    cond,
    database,
    neighbour_ids,
    owner_map,
    norm_gain,
    w_query_enc,
    w_out_enc,
    w_key_dec,
    w_value_dec,
    cotangent,
):
    return fused(
        neighbour_ids.T,
        owner_map.T,
        database,
        cond,
        norm_gain.reshape(1, -1),
        w_query_enc,
        w_out_enc,
        w_key_dec,
        w_value_dec,
        queries,
        cotangent,
    )


def solution(mesh):
    tokens = P(("seq", "enc"), None)
    return jax.shard_map(
        body,
        mesh=mesh,
        in_specs=(tokens, tokens, P("enc", None, None), tokens, tokens, P(), P(), P(), P(), P(), tokens),
        out_specs=(tokens,) * 7,
        check_vma=False,
    )
```

```python
import functools

import jax
import jax.numpy as jnp
from jax import lax
from jax.experimental import pallas as pl
from jax.experimental.pallas import tpu as pltpu
from jax.sharding import PartitionSpec as P

EPS = 1e-06
MESH = pl.DeviceIdType.MESH

F32, BF16 = jnp.float32, jnp.bfloat16
AXES = ("x", "y", "z")
TILES = 9
WHOLE_SLOTS = (
    (1, 2, 3, 4, 5, 6, 7, 8, 14),
    (5, 6, 7, 8, 9, 11, 12, 14, 17),
    (7, 8, 9, 10, 12, 13, 14, 16, 19),
    (9, 10, 11, 13, 14, 15, 16, 18, 21),
)
HALF_SLOTS = ((15, 16), (17, 18), (19, 20), (21, 22))
STEPS = 23
FIRST_AXES = (2, 0, 1, 2, 0, 2, 1, 2, 0)
HALF_SLOTS = ((15, 16), (17, 18), (19, 20), (21, 22))
SERVERS = ((0, 0), (0, 1), (1, 0), (1, -1), (2, 0), (2, 1), (3, 0), (3, -1))


def place():
    s, e = lax.axis_index("seq"), lax.axis_index("enc")
    return dict(core=s % 2, z=(s // 2) % 4, y=(s // 8) * 2 + e % 2, x=e // 2)


def device_of(at):
    y = at["y"]
    return ((y // 2) * 8 + at["z"] * 2 + at["core"], at["x"] * 2 + y % 2)


def moved(at, **steps):
    there = dict(at)
    for axis, step in steps.items():
        there[axis] = (at[axis] + step) % (2 if axis == "core" else 4)
    return there


def along(steps):
    p = (lax.axis_index("seq") * 8 + lax.axis_index("enc") + steps) % 128
    return (p // 8, p % 8)


def pick(index, values):
    if isinstance(index, int):
        return values[index]
    return jnp.where(index == 0, values[0], jnp.where(index == 1, values[1], values[2]))


def rows_of(axis, v):
    return ((0, 2 * v), (v // 2 * 4, v % 2), (v, 0))[axis]


def pick_pair(index, pairs):
    return tuple(pick(index, [pair[i] for pair in pairs]) for i in (0, 1))


class Map:
    def __init__(self):
        at = self.at = place()
        self.core = at["core"]
        self.other_core = device_of(moved(at, core=1))
        self.devices = [[device_of(moved(at, **{a: r})) for a in AXES] for r in range(4)]
        self.values = [[(at[a] + r) % 4 for a in AXES] for r in range(4)]
        self.places = [[rows_of(i, each[i]) for i in range(3)] for each in self.values]
        self.before, self.after = along(-1), along(1)


def remote(src, dst, send, recv, device):
    return pltpu.make_async_remote_copy(
        src_ref=src, dst_ref=dst, send_sem=send, recv_sem=recv, device_id=device, device_id_type=MESH
    )


def dot(a, b):
    return jnp.dot(a, b, preferred_element_type=F32)


def dot_nt(a, b):
    return lax.dot_general(a, b, (((1,), (1,)), ((), ())), preferred_element_type=F32)


def dot_tn(a, b):
    return lax.dot_general(a, b, (((0,), (0,)), ((), ())), preferred_element_type=F32)


class Tile:
    def __init__(self, map, t, turn, grads, came, sends, gets, kept, ssem, rsem, put):
        self.map, self.t, self.grads, self.came = map, t, grads, came
        self.sends, self.gets, self.kept = sends, gets, kept
        self.ssem, self.rsem, self.put = ssem, rsem, put
        if isinstance(turn, int):
            self.axes = [(turn + i) % 3 for i in range(3)]
        else:
            self.axes = [turn, jnp.where(turn == 2, 0, turn + 1), jnp.where(turn == 0, 2, turn - 1)]

    def value(self, level, r):
        return pick(self.axes[level], self.map.values[r])

    def copy(self, level, r=1):
        if level == 0:
            device, src, dst, sem = self.map.other_core, self.outgoing(), self.came, 0
        else:
            device = pick_pair(self.axes[level - 1], self.map.devices[r])
            src, dst, sem = self.sends[level - 1].at[r - 1], self.gets[level - 1].at[r - 1], 3 * level - 3 + r
        return remote(src, dst, self.ssem.at[self.t, sem], self.rsem.at[self.t, sem], device)

    def start(self):
        self.copy(0).start()

    def take(self, level):
        if level == 0:
            self.copy(0).wait_recv()
        else:
            for r in (1, 2, 3):
                self.copy(level, r).wait_recv()
        (self.take_core, self.take_first, self.take_second, self.take_third)[level]()

    def take_core(self):
        each = [
            [pick_pair(self.axes[level], [rows_of(a, v) for a in range(3)]) for v in range(4)] for level in (1, 2)
        ]
        rest = [tuple(a + b for a, b in zip(each[0][i // 4], each[1][i % 4])) for i in range(16)]
        for r in (2, 1, 3, 0):
            high, low = pick_pair(self.axes[0], self.map.places[r])
            for i in range(16):
                value = self.pair(high + rest[i][0], low + rest[i][1])
                if r:
                    self.sends[0][r - 1, i] = self.lower(value)
                else:
                    self.kept[0][i] = value
            if r:
                self.copy(1, r).start()
        self.copy(0).wait_send()

    def take_first(self):
        for r in (2, 1, 3, 0):
            first = self.value(1, r) * 4
            for i in range(4):
                c = first + i
                got = [self.higher(self.gets[0][q, c]) for q in range(3)]
                value = self.kept[0][c] + got[0] + got[1] + got[2]
                if r:
                    self.sends[1][r - 1, i] = value.astype(self.sends[1].dtype)
                else:
                    self.kept[1][i] = value
            if r:
                self.copy(2, r).start()

    def take_second(self):
        for r in (2, 1, 3, 0):
            c = self.value(2, r)
            got = [self.gets[1][q, c].astype(F32) for q in range(3)]
            value = self.kept[1][c] + got[0] + got[1] + got[2]
            if r:
                self.sends[2][r - 1, 0] = value.astype(self.sends[2].dtype)
                self.copy(3, r).start()
            else:
                self.kept[2][0] = value

    def take_third(self):
        got = [self.gets[2][q, 0].astype(F32) for q in range(3)]
        self.put(self.kept[2][0] + got[0] + got[1] + got[2])
        for level in (1, 2, 3):
            for r in (1, 2, 3):
                self.copy(level, r).wait_send()


class PairTile(Tile):
    def outgoing(self):
        return self.grads.at[:, :, 1 - self.map.core]

    def pair(self, high, low):
        core = self.map.core
        parts = [self.grads[i, high, core, low] + self.came[i, high, low] for i in (0, 1)]
        return jnp.concatenate(parts, axis=0)

    def lower(self, value):
        return value.astype(BF16)

    def higher(self, value):
        return value.astype(F32)


class HalfTile(Tile):
    def outgoing(self):
        return self.grads.at[:, 1 - self.map.core]

    def pair(self, high, low):
        return self.grads[high, self.map.core, low] + self.came[high, low]

    def lower(self, value):
        return jnp.concatenate([value[:, :128], value[:, 128:]], axis=0).astype(BF16)

    def higher(self, value):
        wide = value.astype(F32)
        return jnp.concatenate([wide[:8], wide[8:]], axis=1)


def by_head(x, reduce, neutral):
    low = lax.broadcasted_iota(jnp.int32, (x.shape[0], 128), 1) < 64
    parts = []
    for t in range(x.shape[1] // 128):
        one = x[:, t * 128 : t * 128 + 128]
        left = reduce(jnp.where(low, one, neutral), axis=-1, keepdims=True)
        right = reduce(jnp.where(low, neutral, one), axis=-1, keepdims=True)
        parts.append(jnp.where(low, left, right))
    return jnp.concatenate(parts, axis=1)


def head_blocks(x):
    wide = x.astype(F32)
    head = lax.broadcasted_iota(jnp.int32, x.shape, 1) // 64
    return jnp.concatenate([jnp.where(head == h, wide, 0.0) for h in range(4)], axis=0).astype(BF16)


def head_diagonal(x):
    head = lax.broadcasted_iota(jnp.int32, (64, 256), 1) // 64
    return sum(jnp.where(head == h, x[h * 64 : h * 64 + 64], 0.0) for h in range(4))


def two_heads(x):
    none = jnp.zeros((x.shape[0], 128), x.dtype)
    return jnp.concatenate(
        [jnp.concatenate([x[:, :128], none], axis=1), jnp.concatenate([none, x[:, 128:]], axis=1)], axis=0
    )


def own_heads(x):
    return jnp.concatenate([x[:64, :128], x[64:, 128:]], axis=1)


def main_kernel(
    ids, owners, database, cond_in, gain, wq_in, wo_in, wk_in, wv_in, q_in, g_in,
    att, dq_out, dcond, gq_out, go_out, gk_out, gv_out,
    pool, cond, wq, wo, wk, wv, q_ref, g_ref,
    asked, asks, blocks_out, upper_rows, lower_rows, later,
    normed, query, probs, mixed, src, kv, dmix, last, first,
    grads, came, send1, get1, send2, get2, send3, get3, kept1, kept2, kept3,
    hcame, hsend1, hget1, hsend2, hget2, hsend3, hget3, hkept1, hkept2, hkept3,
    load_sem, ask_s, ask_r, block_s, block_r, ahead_s, ahead_r, shift_s, shift_r, ssem, rsem,
):
    map = Map()
    at = map.at
    me = lax.axis_index("seq") * 8 + lax.axis_index("enc")
    loads = [
        pltpu.make_async_copy(a, b, load_sem.at[i])
        for i, (a, b) in enumerate(
            (
                (database, pool), (cond_in, cond), (wq_in, wq), (wo_in, wo),
                (wk_in, wk), (wv_in, wv), (q_in, q_ref), (g_in, g_ref),
            )
        )
    ]
    loads[0].start()

    barrier = pltpu.get_barrier_semaphore()
    steps = {(dx * s % 4, dy * s % 4) for dx, dy in SERVERS for s in (1, -1)} | {(0, 2)}
    steps = sorted(steps - {(0, 0)})
    peers = [device_of(moved(at, x=dx, y=dy)) for dx, dy in steps]
    peers += [device_of(moved(at, core=1))] + [device_of(moved(at, z=r)) for r in (1, 2, 3)]
    peers += [map.before, map.after]
    for peer in peers:
        pl.semaphore_signal(barrier, inc=1, device_id=peer, device_id_type=MESH)
    pl.semaphore_wait(barrier, len(peers))

    server = [((at["x"] + dx) % 4) * 2 + (at["y"] + dy) % 2 for dx, dy in SERVERS]

    def row_at(r):
        each = [(owners[j, s], ids[j, s]) for s in range(3) for j in range(2)]
        return sum(jnp.where(owner == server[r], row, 0) for owner, row in each)

    asking, answers = [], []
    for r in (5, 7, 3, 4, 2, 6, 1):
        dx, dy = SERVERS[r]
        asks[r] = jnp.full((8, 128), row_at(r), jnp.int32)
        copy = remote(
            asks.at[r], asked.at[r], ask_s.at[r], ask_r.at[r], device_of(moved(at, x=dx, y=dy))
        )
        copy.start()
        asking.append((r, copy))
    for copy in loads[1:]:
        copy.start()
    loads[0].wait()
    blocks = (upper_rows, lower_rows)
    for h in range(2):
        part = pl.ds(h * 64, 64)
        for r, copy in asking:
            dx, dy = SERVERS[r]
            if h == 0:
                copy.wait_recv()
                blocks_out[r] = pool[jnp.max(asked[r])]
            answer = remote(
                blocks_out.at[r, part], blocks[h].at[r], block_s.at[h, r], block_r.at[h, r],
                device_of(moved(at, x=-dx, y=-dy)),
            )
            answer.start()
            answers.append(answer)
    own = pool[row_at(0)]
    for h in range(2):
        blocks[h][0] = own[h * 64 : h * 64 + 64]
    for r, copy in asking:
        copy.wait_send()
    for copy in loads[1:4]:
        copy.wait()
    slots = [
        [sum(jnp.where(owners[j, s] == server[r], r, 0) for r in range(1, 8)) for j in range(2)] for s in range(3)
    ]

    def encode(h):
        low = h * 384
        both = slice(low, low + 384)
        for s in range(3):
            for j in range(2):
                at_rows = slice(low + s * 128 + j * 64, low + s * 128 + j * 64 + 64)
                raw = blocks[h][slots[s][j]].astype(F32)
                inverse = lax.rsqrt(jnp.mean(raw * raw, axis=-1, keepdims=True) + EPS)
                normed[at_rows, :] = (raw * inverse * gain[...]).astype(BF16)
        query[both, :] = dot(normed[both, :], wq[...]).astype(BF16)
        pieces = [(s, slice(c * 256, c * 256 + 256)) for s in range(3) for c in range(2)]
        here = [slice(low + s * 128, low + s * 128 + 128) for s in range(3)]
        span = [slice(s * 64, s * 64 + 64) for s in range(3)]
        k4 = [head_blocks(cond[span[s], c]) for s, c in pieces]
        v4 = [head_blocks(cond[span[s], c.start + 512 : c.stop + 512]) for s, c in pieces]
        scores = [dot_nt(query[here[s], c], k) * 0.125 for (s, c), k in zip(pieces, k4)]
        e = [jnp.exp(x - by_head(x, jnp.max, -jnp.inf)) for x in scores]
        p = [x / by_head(x, jnp.sum, 0.0) for x in e]
        for (s, c), x, v in zip(pieces, p, v4):
            probs[here[s], c] = x
            mixed[here[s], c] = dot(x.astype(BF16), v).astype(BF16)
        out = dot(mixed[both, :], wo[...])
        for s in range(3):
            for j in range(2):
                i = s * 128 + j * 64
                raw = blocks[h][slots[s][j]].astype(F32)
                src[low + i : low + i + 64, :] = (raw + out[i : i + 64]).astype(BF16)

    for answer in answers[:7]:
        answer.wait_recv()
    encode(0)
    for answer in answers[7:]:
        answer.wait_recv()

    def ahead(t):
        cols = pl.ds(pl.multiple_of(t * 256, 256), 256)
        return [
            remote(
                ref.at[pl.ds(0, 64), cols], later.at[i, :, cols], ahead_s.at[i, t], ahead_r.at[i, t], map.before
            )
            for i, ref in enumerate((q_in, g_in))
        ]

    def send_ahead(t, _):
        for copy in ahead(t):
            copy.start()
        return 0

    lax.fori_loop(0, 8, send_ahead, 0)
    encode(1)
    for copy in loads[4:]:
        copy.wait()
    for answer in answers:
        answer.wait_send()
    followed = jnp.where(me == 127, 0.0, 1.0).astype(BF16)

    def whole_tile(t):
        def put(total):
            def sheets():
                cols = pl.ds(pl.multiple_of(t * 256, 256), 256)
                gk_out[:, cols] = total[:8]
                gv_out[:, cols] = total[8:]

            def outer():
                for j in range(4):
                    go_out[:, j * 256 : j * 256 + 256] = total[j * 4 : j * 4 + 4]

            pl.when(t < 8)(sheets)
            pl.when(t == 8)(outer)

        turn = sum(jnp.where(t == i, a, 0) for i, a in enumerate(FIRST_AXES) if a)
        return PairTile(
            map, t, turn, grads.at[t % 3], came.at[t % 4],
            (send1.at[t], send2.at[t], send3.at[t]), (get1.at[t], get2.at[t], get3.at[t]),
            (kept1.at[t], kept2.at[t], kept3.at[t]), ssem, rsem, put,
        )

    def half_tile(i):
        def put(total):
            gq_out[:, pl.ds(pl.multiple_of(i * 256, 256), 256)] = total

        return HalfTile(
            map, TILES + i, 1 + i, grads.at[0, i], hcame.at[i],
            (hsend1.at[i], hsend2.at[i], hsend3.at[i]), (hget1.at[i], hget2.at[i], hget3.at[i]),
            (hkept1.at[i], hkept2.at[i], hkept3.at[i]), ssem, rsem, put,
        )

    scale = 128 ** (-0.5)

    def onward(t):
        cols = pl.ds(pl.multiple_of(t * 256, 256), 256)
        return [
            remote(last.at[i, :, cols], first.at[i, :, cols], shift_s.at[i, t], shift_r.at[i, t], map.after)
            for i in range(2)
        ]

    def of_span(ref, s, cols):
        return jnp.concatenate([ref[h * 384 + s * 128 : h * 384 + s * 128 + 128, cols] for h in range(2)], axis=0)

    def half_rows(t):
        return t // 4 * 6, pl.ds(pl.multiple_of(t % 4 * 256, 256), 256)

    def decode(t):
        cols = pl.ds(pl.multiple_of(t * 256, 256), 256)
        base, pool_cols = half_rows(t)
        for copy in ahead(t):
            copy.wait()
        kv[0] = dot(src[...], wk[:, cols]).astype(BF16)
        kv[1] = dot(src[...], wv[:, cols]).astype(BF16)
        k, v = ([of_span(kv.at[i], s, slice(None)) for s in range(3)] for i in range(2))
        afters = [slice(s * 64 + 64, s * 64 + 128) for s in range(3)]
        q2 = [two_heads(q_ref[a, cols]) for a in afters[:2]] + [two_heads(later[0, :, cols] * followed)]
        g2 = [two_heads(g_ref[a, cols]) for a in afters[:2]] + [two_heads(later[1, :, cols] * followed)]
        scores = [dot_nt(q2[s], k[s]) * scale for s in range(3)]
        dw = [dot_nt(g2[s], v[s]) for s in range(3)]
        e = [jnp.exp(x - jnp.max(x, axis=-1, keepdims=True)) for x in scores]
        p = [x / jnp.sum(x, axis=-1, keepdims=True) for x in e]
        w = [x.astype(BF16) for x in p]
        o = [own_heads(dot(w[s], v[s])).astype(BF16) for s in range(3)]
        dv = [dot_tn(w[s], g2[s]).astype(BF16) for s in range(3)]
        ds = [
            (p[s] * (dw[s] - jnp.sum(dw[s] * p[s], axis=-1, keepdims=True)) * scale).astype(BF16) for s in range(3)
        ]
        dq = [own_heads(dot(ds[s], k[s])).astype(BF16) for s in range(3)]
        dk = [dot_tn(ds[s], q2[s]).astype(BF16) for s in range(3)]
        for s in range(3):
            if s < 2:
                att[afters[s], cols] = o[s]
                dq_out[afters[s], cols] = dq[s]
            else:
                last[0, :, cols] = o[s]
                last[1, :, cols] = dq[s]
            for h in range(2):
                pool[base + h * 3 + s, :, pool_cols] = dk[s][h * 128 : h * 128 + 128]
                pool[base + h * 3 + s + 12, :, pool_cols] = dv[s][h * 128 : h * 128 + 128]
        for i in range(2):
            sheet = dot_tn(src[...], pool[pl.ds(base + 12 * i, 6), :, pool_cols].reshape(768, 256))
            grads[t % 3, i] = sheet.reshape(8, 2, 8, 8, 256)
        for copy in onward(t):
            copy.start()

    def sources_back(i):
        cols = pl.ds(pl.multiple_of(i * 256, 256), 256)
        total = sum(
            dot_nt(pool[j * 6 : j * 6 + 6].reshape(768, 1024), w[cols, j % 2 * 1024 : j % 2 * 1024 + 1024])
            for j, w in enumerate((wk, wk, wv, wv))
        )
        pool[24:30, :, cols] = total.astype(BF16).reshape(6, 128, 256)

    def outer_out():
        for i in range(2):
            for j in range(2):
                cols = slice(i * 512 + j * 256, i * 512 + j * 256 + 256)
                sheet = dot_tn(mixed[...], pool[24:30, :, cols].reshape(768, 256))
                grads[1, j, 0:4] = sheet.reshape(4, 2, 8, 8, 256)

            def stack(g, _, i=i):
                for q in range(8):
                    left, right = (grads[1, j, g // 2, g % 2, q] for j in (0, 1))
                    for upper in range(2):
                        rows = slice(upper * 4, upper * 4 + 4)
                        p = 2 * q + upper
                        grads[2, i, g, p // 8, p % 8] = jnp.concatenate([left[rows], right[rows]], axis=0)
                return 0

            lax.fori_loop(0, 8, stack, 0)
        whole_tile(8).start()

    def mixed_back():
        dmix[...] = dot_nt(pool[24:30].reshape(768, 1024), wo[...]).astype(BF16)

    def query_back(half):
        cols = pl.ds(pl.multiple_of(half * 256, 256), 256)
        vcols = pl.ds(pl.multiple_of(half * 256 + 512, 256), 256)
        spans = [slice(s * 64, s * 64 + 64) for s in range(3)]
        k4 = [head_blocks(cond[span, cols]) for span in spans]
        v4 = [head_blocks(cond[span, vcols]) for span in spans]
        dw = [dot_nt(of_span(dmix, s, cols), v4[s]) for s in range(3)]
        p = [of_span(probs, s, cols) for s in range(3)]
        sums = [by_head(dw[s] * p[s], jnp.sum, 0.0) for s in range(3)]
        ds = [(p[s] * (dw[s] - sums[s]) * 0.125).astype(BF16) for s in range(3)]
        for s in range(3):
            dquery = dot(ds[s], k4[s]).astype(BF16)
            for h in range(2):
                rows, part = pl.ds(h * 384 + s * 128, 128), slice(h * 128, h * 128 + 128)
                mixed[rows, cols] = ds[s][part]
                kv[half, rows, :] = dquery[part]
        grads[0, half] = dot_tn(normed[...], kv[half]).reshape(8, 2, 8, 8, 256)
        half_tile(half).start()

    def cond_back():
        def some(i, _):
            s, half = i // 2, i % 2
            span = pl.ds(pl.multiple_of(s * 64, 64), 64)
            cols = pl.ds(pl.multiple_of(half * 256, 256), 256)
            vcols = pl.ds(pl.multiple_of(half * 256 + 512, 256), 256)

            def both(ref):
                parts = [ref[pl.ds(pl.multiple_of(h * 384 + s * 128, 128), 128), cols] for h in range(2)]
                return jnp.concatenate(parts, axis=0)

            w = both(probs).astype(BF16)
            dcond[span, vcols] = head_diagonal(dot_tn(w, both(dmix))).astype(BF16)
            dcond[span, cols] = head_diagonal(dot_tn(both(mixed), both(query))).astype(BF16)
            return 0

        lax.fori_loop(0, 6, some, 0)

    def tile_at(slot, slots):
        return sum(jnp.where(slot == at_slot, t + 1, 0) for t, at_slot in enumerate(slots)) - 1

    def step(slot, _):
        pl.when(slot < 8)(lambda: decode(slot))
        pl.when((slot >= 8) & (slot < 12))(lambda: sources_back(slot - 8))
        pl.when(slot == 12)(outer_out)
        pl.when(slot == 13)(mixed_back)
        pl.when((slot == 14) | (slot == 15))(lambda: query_back(slot - 14))
        pl.when(slot == 16)(cond_back)
        def take_halves(levels):
            for level in levels:
                i = tile_at(slot, HALF_SLOTS[level])
                pl.when(i >= 0)(lambda i=i, level=level: half_tile(i).take(level))

        take_halves((3, 2, 1))
        for level in (3, 2, 1, 0):
            t = tile_at(slot, WHOLE_SLOTS[level])
            pl.when(t >= 0)(lambda t=t, level=level: whole_tile(t).take(level))
        take_halves((0,))
        pl.when(slot < 8)(lambda: whole_tile(slot).start())
        return 0

    lax.fori_loop(0, STEPS, step, 0)

    def arrive(t, _):
        for copy in onward(t):
            copy.wait()
        return 0

    lax.fori_loop(0, 8, arrive, 0)
    followed_by = jnp.where(me == 0, 0.0, 1.0).astype(BF16)
    att[:64, :] = first[0] * followed_by
    dq_out[:64, :] = first[1] * followed_by


def fused(ids, owners, database, cond, gain, wq, wo, wk, wv, queries, grads):
    vmem, smem = pl.BlockSpec(memory_space=pltpu.VMEM), pl.BlockSpec(memory_space=pltpu.SMEM)
    hbm = pl.BlockSpec(memory_space=pl.ANY)
    shape, dma = jax.ShapeDtypeStruct, pltpu.SemaphoreType.DMA
    half = lambda *dims: pltpu.VMEM(dims, BF16)
    full = lambda *dims: pltpu.VMEM(dims, F32)
    outs = pl.pallas_call(
        main_kernel,
        out_shape=(
            shape((192, 2048), BF16),
            shape((192, 2048), BF16),
            shape((192, 1024), BF16),
            shape((8, 512), F32),
            shape((4, 1024), F32),
            shape((8, 2048), F32),
            shape((8, 2048), F32),
        ),
        in_specs=[smem, smem, hbm, hbm, vmem] + [hbm] * 6,
        out_specs=(vmem,) * 7,
        scratch_shapes=[
            half(32, 128, 1024), half(192, 1024), half(1024, 512), half(512, 1024),
            half(1024, 2048), half(1024, 2048), half(192, 2048), half(192, 2048),
            pltpu.VMEM((8, 8, 128), jnp.int32), pltpu.VMEM((8, 8, 128), jnp.int32),
            half(8, 128, 1024), half(8, 64, 1024), half(8, 64, 1024), half(2, 64, 2048),
            half(768, 1024), half(768, 512), full(768, 512), half(768, 512), half(768, 1024),
            half(2, 768, 256), half(768, 512),
            half(2, 64, 2048), half(2, 64, 2048),
            full(3, 2, 8, 2, 8, 8, 256), full(4, 2, 8, 8, 8, 256),
            half(TILES, 3, 16, 16, 256), half(TILES, 3, 16, 16, 256),
            half(TILES, 3, 4, 16, 256), half(TILES, 3, 4, 16, 256),
            half(TILES, 3, 1, 16, 256), half(TILES, 3, 1, 16, 256),
            full(TILES, 16, 16, 256), full(TILES, 4, 16, 256), full(TILES, 1, 16, 256),
            full(2, 8, 8, 8, 256), half(2, 3, 16, 16, 128), half(2, 3, 16, 16, 128),
            full(2, 3, 4, 8, 256), full(2, 3, 4, 8, 256), full(2, 3, 1, 8, 256), full(2, 3, 1, 8, 256),
            full(2, 16, 8, 256), full(2, 4, 8, 256), full(2, 1, 8, 256),
            dma((8,)), dma((8,)), dma((8,)), dma((2, 8)), dma((2, 8)), dma((2, 8)), dma((2, 8)), dma((2, 8)), dma((2, 8)),
            dma((TILES + 2, 10)), dma((TILES + 2, 10)),
        ],
        compiler_params=pltpu.CompilerParams(
            collective_id=0, has_side_effects=True, vmem_limit_bytes=63 * 1024 * 1024
        ),
    )(ids, owners, database, cond, gain, wq, wo, wk, wv, queries, grads)

    def leave(*refs):
        n, sem = len(outs), refs[-1]
        copies = [pltpu.make_async_copy(refs[i], refs[n + i], sem.at[i]) for i in range(n)]
        for copy in copies:
            copy.start()
        for copy in copies:
            copy.wait()

    return pl.pallas_call(
        leave,
        out_shape=tuple(shape(o.shape, o.dtype) for o in outs),
        in_specs=[hbm] * len(outs),
        out_specs=(vmem,) * len(outs),
        scratch_shapes=[dma((len(outs),))],
    )(*outs)


def body(
    queries,
    cond,
    database,
    neighbour_ids,
    owner_map,
    norm_gain,
    w_query_enc,
    w_out_enc,
    w_key_dec,
    w_value_dec,
    cotangent,
):
    return fused(
        neighbour_ids.T,
        owner_map.T,
        database,
        cond,
        norm_gain.reshape(1, -1),
        w_query_enc,
        w_out_enc,
        w_key_dec,
        w_value_dec,
        queries,
        cotangent,
    )


def solution(mesh):
    tokens = P(("seq", "enc"), None)
    return jax.shard_map(
        body,
        mesh=mesh,
        in_specs=(tokens, tokens, P("enc", None, None), tokens, tokens, P(), P(), P(), P(), P(), tokens),
        out_specs=(tokens,) * 7,
        check_vma=False,
    )
```

```python
import functools

import jax
import jax.numpy as jnp
from jax import lax
from jax.experimental import pallas as pl
from jax.experimental.pallas import tpu as pltpu
from jax.sharding import PartitionSpec as P

EPS = 1e-06
MESH = pl.DeviceIdType.MESH

F32, BF16 = jnp.float32, jnp.bfloat16
AXES = ("x", "y", "z")
TILES = 9
WHOLE_SLOTS = (
    (2, 3, 4, 5, 6, 7, 8, 9, 14),
    (6, 7, 8, 10, 11, 13, 15, 16, 18),
    (8, 9, 11, 13, 14, 16, 17, 18, 20),
    (10, 12, 14, 16, 17, 18, 19, 21, 22),
)
HALF_SLOTS = ((15, 16), (17, 18), (19, 20), (21, 22))
STEPS = 23
FIRST_AXES = (2, 0, 1, 2, 0, 2, 1, 2, 0)
HALF_SLOTS = ((15, 16), (17, 18), (19, 20), (21, 22))
SERVERS = ((0, 0), (0, 1), (1, 0), (1, -1), (2, 0), (2, 1), (3, 0), (3, -1))


def place():
    s, e = lax.axis_index("seq"), lax.axis_index("enc")
    return dict(core=s % 2, z=(s // 2) % 4, y=(s // 8) * 2 + e % 2, x=e // 2)


def device_of(at):
    y = at["y"]
    return ((y // 2) * 8 + at["z"] * 2 + at["core"], at["x"] * 2 + y % 2)


def moved(at, **steps):
    there = dict(at)
    for axis, step in steps.items():
        there[axis] = (at[axis] + step) % (2 if axis == "core" else 4)
    return there


def along(steps):
    p = (lax.axis_index("seq") * 8 + lax.axis_index("enc") + steps) % 128
    return (p // 8, p % 8)


def pick(index, values):
    if isinstance(index, int):
        return values[index]
    return jnp.where(index == 0, values[0], jnp.where(index == 1, values[1], values[2]))


def rows_of(axis, v):
    return ((0, 2 * v), (v // 2 * 4, v % 2), (v, 0))[axis]


def pick_pair(index, pairs):
    return tuple(pick(index, [pair[i] for pair in pairs]) for i in (0, 1))


class Map:
    def __init__(self):
        at = self.at = place()
        self.core = at["core"]
        self.other_core = device_of(moved(at, core=1))
        self.devices = [[device_of(moved(at, **{a: r})) for a in AXES] for r in range(4)]
        self.values = [[(at[a] + r) % 4 for a in AXES] for r in range(4)]
        self.places = [[rows_of(i, each[i]) for i in range(3)] for each in self.values]
        self.before, self.after = along(-1), along(1)


def remote(src, dst, send, recv, device):
    return pltpu.make_async_remote_copy(
        src_ref=src, dst_ref=dst, send_sem=send, recv_sem=recv, device_id=device, device_id_type=MESH
    )


def dot(a, b):
    return jnp.dot(a, b, preferred_element_type=F32)


def dot_nt(a, b):
    return lax.dot_general(a, b, (((1,), (1,)), ((), ())), preferred_element_type=F32)


def dot_tn(a, b):
    return lax.dot_general(a, b, (((0,), (0,)), ((), ())), preferred_element_type=F32)


class Tile:
    def __init__(self, map, t, turn, grads, came, sends, gets, kept, ssem, rsem, put):
        self.map, self.t, self.grads, self.came = map, t, grads, came
        self.sends, self.gets, self.kept = sends, gets, kept
        self.ssem, self.rsem, self.put = ssem, rsem, put
        if isinstance(turn, int):
            self.axes = [(turn + i) % 3 for i in range(3)]
        else:
            self.axes = [turn, jnp.where(turn == 2, 0, turn + 1), jnp.where(turn == 0, 2, turn - 1)]

    def value(self, level, r):
        return pick(self.axes[level], self.map.values[r])

    def copy(self, level, r=1):
        if level == 0:
            device, src, dst, sem = self.map.other_core, self.outgoing(), self.came, 0
        else:
            device = pick_pair(self.axes[level - 1], self.map.devices[r])
            src, dst, sem = self.sends[level - 1].at[r - 1], self.gets[level - 1].at[r - 1], 3 * level - 3 + r
        return remote(src, dst, self.ssem.at[self.t, sem], self.rsem.at[self.t, sem], device)

    def start(self):
        self.copy(0).start()

    def take(self, level):
        if level == 0:
            self.copy(0).wait_recv()
        else:
            for r in (1, 2, 3):
                self.copy(level, r).wait_recv()
        (self.take_core, self.take_first, self.take_second, self.take_third)[level]()

    def take_core(self):
        each = [
            [pick_pair(self.axes[level], [rows_of(a, v) for a in range(3)]) for v in range(4)] for level in (1, 2)
        ]
        rest = [tuple(a + b for a, b in zip(each[0][i // 4], each[1][i % 4])) for i in range(16)]
        for r in (2, 1, 3, 0):
            high, low = pick_pair(self.axes[0], self.map.places[r])
            for i in range(16):
                value = self.pair(high + rest[i][0], low + rest[i][1])
                if r:
                    self.sends[0][r - 1, i] = self.lower(value)
                else:
                    self.kept[0][i] = value
            if r:
                self.copy(1, r).start()
        self.copy(0).wait_send()

    def take_first(self):
        for r in (2, 1, 3, 0):
            first = self.value(1, r) * 4
            for i in range(4):
                c = first + i
                got = [self.higher(self.gets[0][q, c]) for q in range(3)]
                value = self.kept[0][c] + got[0] + got[1] + got[2]
                if r:
                    self.sends[1][r - 1, i] = value.astype(self.sends[1].dtype)
                else:
                    self.kept[1][i] = value
            if r:
                self.copy(2, r).start()

    def take_second(self):
        for r in (2, 1, 3, 0):
            c = self.value(2, r)
            got = [self.gets[1][q, c].astype(F32) for q in range(3)]
            value = self.kept[1][c] + got[0] + got[1] + got[2]
            if r:
                self.sends[2][r - 1, 0] = value.astype(self.sends[2].dtype)
                self.copy(3, r).start()
            else:
                self.kept[2][0] = value

    def take_third(self):
        got = [self.gets[2][q, 0].astype(F32) for q in range(3)]
        self.put(self.kept[2][0] + got[0] + got[1] + got[2])
        for level in (1, 2, 3):
            for r in (1, 2, 3):
                self.copy(level, r).wait_send()


class PairTile(Tile):
    def outgoing(self):
        return self.grads.at[:, :, 1 - self.map.core]

    def pair(self, high, low):
        core = self.map.core
        parts = [self.grads[i, high, core, low] + self.came[i, high, low] for i in (0, 1)]
        return jnp.concatenate(parts, axis=0)

    def lower(self, value):
        return value.astype(BF16)

    def higher(self, value):
        return value.astype(F32)


class HalfTile(Tile):
    def outgoing(self):
        return self.grads.at[:, 1 - self.map.core]

    def pair(self, high, low):
        return self.grads[high, self.map.core, low] + self.came[high, low]

    def lower(self, value):
        return jnp.concatenate([value[:, :128], value[:, 128:]], axis=0).astype(BF16)

    def higher(self, value):
        wide = value.astype(F32)
        return jnp.concatenate([wide[:8], wide[8:]], axis=1)


def by_head(x, reduce, neutral):
    low = lax.broadcasted_iota(jnp.int32, (x.shape[0], 128), 1) < 64
    parts = []
    for t in range(x.shape[1] // 128):
        one = x[:, t * 128 : t * 128 + 128]
        left = reduce(jnp.where(low, one, neutral), axis=-1, keepdims=True)
        right = reduce(jnp.where(low, neutral, one), axis=-1, keepdims=True)
        parts.append(jnp.where(low, left, right))
    return jnp.concatenate(parts, axis=1)


def head_blocks(x):
    wide = x.astype(F32)
    head = lax.broadcasted_iota(jnp.int32, x.shape, 1) // 64
    return jnp.concatenate([jnp.where(head == h, wide, 0.0) for h in range(4)], axis=0).astype(BF16)


def head_diagonal(x):
    head = lax.broadcasted_iota(jnp.int32, (64, 256), 1) // 64
    return sum(jnp.where(head == h, x[h * 64 : h * 64 + 64], 0.0) for h in range(4))


def two_heads(x):
    none = jnp.zeros((x.shape[0], 128), x.dtype)
    return jnp.concatenate(
        [jnp.concatenate([x[:, :128], none], axis=1), jnp.concatenate([none, x[:, 128:]], axis=1)], axis=0
    )


def own_heads(x):
    return jnp.concatenate([x[:64, :128], x[64:, 128:]], axis=1)


def main_kernel(
    ids, owners, database, cond_in, gain, wq_in, wo_in, wk_in, wv_in, q_in, g_in,
    att, dq_out, dcond, gq_out, go_out, gk_out, gv_out,
    pool, cond, wq, wo, wk, wv, q_ref, g_ref,
    asked, asks, blocks_out, upper_rows, lower_rows, later,
    normed, query, probs, mixed, src, kv, dmix, last, first,
    grads, came, send1, get1, send2, get2, send3, get3, kept1, kept2, kept3,
    hcame, hsend1, hget1, hsend2, hget2, hsend3, hget3, hkept1, hkept2, hkept3,
    load_sem, ask_s, ask_r, block_s, block_r, ahead_s, ahead_r, shift_s, shift_r, ssem, rsem,
):
    map = Map()
    at = map.at
    me = lax.axis_index("seq") * 8 + lax.axis_index("enc")
    loads = [
        pltpu.make_async_copy(a, b, load_sem.at[i])
        for i, (a, b) in enumerate(
            (
                (database, pool), (cond_in, cond), (wq_in, wq), (wo_in, wo),
                (wk_in, wk), (wv_in, wv), (q_in, q_ref), (g_in, g_ref),
            )
        )
    ]
    loads[0].start()

    barrier = pltpu.get_barrier_semaphore()
    steps = {(dx * s % 4, dy * s % 4) for dx, dy in SERVERS for s in (1, -1)} | {(0, 2)}
    steps = sorted(steps - {(0, 0)})
    peers = [device_of(moved(at, x=dx, y=dy)) for dx, dy in steps]
    peers += [device_of(moved(at, core=1))] + [device_of(moved(at, z=r)) for r in (1, 2, 3)]
    peers += [map.before, map.after]
    for peer in peers:
        pl.semaphore_signal(barrier, inc=1, device_id=peer, device_id_type=MESH)
    pl.semaphore_wait(barrier, len(peers))

    server = [((at["x"] + dx) % 4) * 2 + (at["y"] + dy) % 2 for dx, dy in SERVERS]

    def row_at(r):
        each = [(owners[j, s], ids[j, s]) for s in range(3) for j in range(2)]
        return sum(jnp.where(owner == server[r], row, 0) for owner, row in each)

    asking, answers = [], []
    for r in (5, 7, 3, 4, 2, 6, 1):
        dx, dy = SERVERS[r]
        asks[r] = jnp.full((8, 128), row_at(r), jnp.int32)
        copy = remote(
            asks.at[r], asked.at[r], ask_s.at[r], ask_r.at[r], device_of(moved(at, x=dx, y=dy))
        )
        copy.start()
        asking.append((r, copy))
    for copy in loads[1:]:
        copy.start()
    loads[0].wait()
    blocks = (upper_rows, lower_rows)
    for h in range(2):
        part = pl.ds(h * 64, 64)
        for r, copy in asking:
            dx, dy = SERVERS[r]
            if h == 0:
                copy.wait_recv()
                blocks_out[r] = pool[jnp.max(asked[r])]
            answer = remote(
                blocks_out.at[r, part], blocks[h].at[r], block_s.at[h, r], block_r.at[h, r],
                device_of(moved(at, x=-dx, y=-dy)),
            )
            answer.start()
            answers.append(answer)
    own = pool[row_at(0)]
    for h in range(2):
        blocks[h][0] = own[h * 64 : h * 64 + 64]
    for r, copy in asking:
        copy.wait_send()
    for copy in loads[1:4]:
        copy.wait()
    slots = [
        [sum(jnp.where(owners[j, s] == server[r], r, 0) for r in range(1, 8)) for j in range(2)] for s in range(3)
    ]

    def encode(h):
        low = h * 384
        both = slice(low, low + 384)
        for s in range(3):
            for j in range(2):
                at_rows = slice(low + s * 128 + j * 64, low + s * 128 + j * 64 + 64)
                raw = blocks[h][slots[s][j]].astype(F32)
                inverse = lax.rsqrt(jnp.mean(raw * raw, axis=-1, keepdims=True) + EPS)
                normed[at_rows, :] = (raw * inverse * gain[...]).astype(BF16)
        query[both, :] = dot(normed[both, :], wq[...]).astype(BF16)
        pieces = [(s, slice(c * 256, c * 256 + 256)) for s in range(3) for c in range(2)]
        here = [slice(low + s * 128, low + s * 128 + 128) for s in range(3)]
        span = [slice(s * 64, s * 64 + 64) for s in range(3)]
        k4 = [head_blocks(cond[span[s], c]) for s, c in pieces]
        v4 = [head_blocks(cond[span[s], c.start + 512 : c.stop + 512]) for s, c in pieces]
        scores = [dot_nt(query[here[s], c], k) * 0.125 for (s, c), k in zip(pieces, k4)]
        e = [jnp.exp(x - by_head(x, jnp.max, -jnp.inf)) for x in scores]
        p = [x / by_head(x, jnp.sum, 0.0) for x in e]
        for (s, c), x, v in zip(pieces, p, v4):
            probs[here[s], c] = x
            mixed[here[s], c] = dot(x.astype(BF16), v).astype(BF16)
        out = dot(mixed[both, :], wo[...])
        for s in range(3):
            for j in range(2):
                i = s * 128 + j * 64
                raw = blocks[h][slots[s][j]].astype(F32)
                src[low + i : low + i + 64, :] = (raw + out[i : i + 64]).astype(BF16)

    def ahead(t):
        cols = pl.ds(pl.multiple_of(t * 256, 256), 256)
        return [
            remote(
                ref.at[pl.ds(0, 64), cols], later.at[i, :, cols], ahead_s.at[i, t], ahead_r.at[i, t], map.before
            )
            for i, ref in enumerate((q_in, g_in))
        ]

    def send_ahead(t, _):
        for copy in ahead(t):
            copy.start()
        return 0

    def send_all_ahead():
        lax.fori_loop(0, 8, send_ahead, 0)

    pl.when(at["y"] % 2 == 1)(send_all_ahead)
    for answer in answers[:7]:
        answer.wait_recv()
    encode(0)
    for answer in answers[7:]:
        answer.wait_recv()

    pl.when(at["y"] % 2 == 0)(send_all_ahead)
    encode(1)
    for copy in loads[4:]:
        copy.wait()
    for answer in answers:
        answer.wait_send()
    followed = jnp.where(me == 127, 0.0, 1.0).astype(BF16)

    def whole_tile(t):
        def put(total):
            def sheets():
                cols = pl.ds(pl.multiple_of(t * 256, 256), 256)
                gk_out[:, cols] = total[:8]
                gv_out[:, cols] = total[8:]

            def outer():
                for j in range(4):
                    go_out[:, j * 256 : j * 256 + 256] = total[j * 4 : j * 4 + 4]

            pl.when(t < 8)(sheets)
            pl.when(t == 8)(outer)

        turn = sum(jnp.where(t == i, a, 0) for i, a in enumerate(FIRST_AXES) if a)
        return PairTile(
            map, t, turn, grads.at[t % 3], came.at[t % 4],
            (send1.at[t], send2.at[t], send3.at[t]), (get1.at[t], get2.at[t], get3.at[t]),
            (kept1.at[t], kept2.at[t], kept3.at[t]), ssem, rsem, put,
        )

    def half_tile(i):
        def put(total):
            gq_out[:, pl.ds(pl.multiple_of(i * 256, 256), 256)] = total

        return HalfTile(
            map, TILES + i, 1 + i, grads.at[0, i], hcame.at[i],
            (hsend1.at[i], hsend2.at[i], hsend3.at[i]), (hget1.at[i], hget2.at[i], hget3.at[i]),
            (hkept1.at[i], hkept2.at[i], hkept3.at[i]), ssem, rsem, put,
        )

    scale = 128 ** (-0.5)

    def onward(t):
        cols = pl.ds(pl.multiple_of(t * 256, 256), 256)
        return [
            remote(last.at[i, :, cols], first.at[i, :, cols], shift_s.at[i, t], shift_r.at[i, t], map.after)
            for i in range(2)
        ]

    def of_span(ref, s, cols):
        return jnp.concatenate([ref[h * 384 + s * 128 : h * 384 + s * 128 + 128, cols] for h in range(2)], axis=0)

    def half_rows(t):
        return t // 4 * 6, pl.ds(pl.multiple_of(t % 4 * 256, 256), 256)

    def decode(t):
        cols = pl.ds(pl.multiple_of(t * 256, 256), 256)
        base, pool_cols = half_rows(t)
        for copy in ahead(t):
            copy.wait()
        kv[0] = dot(src[...], wk[:, cols]).astype(BF16)
        kv[1] = dot(src[...], wv[:, cols]).astype(BF16)
        k, v = ([of_span(kv.at[i], s, slice(None)) for s in range(3)] for i in range(2))
        afters = [slice(s * 64 + 64, s * 64 + 128) for s in range(3)]
        q2 = [two_heads(q_ref[a, cols]) for a in afters[:2]] + [two_heads(later[0, :, cols] * followed)]
        g2 = [two_heads(g_ref[a, cols]) for a in afters[:2]] + [two_heads(later[1, :, cols] * followed)]
        scores = [dot_nt(q2[s], k[s]) * scale for s in range(3)]
        dw = [dot_nt(g2[s], v[s]) for s in range(3)]
        e = [jnp.exp(x - jnp.max(x, axis=-1, keepdims=True)) for x in scores]
        p = [x / jnp.sum(x, axis=-1, keepdims=True) for x in e]
        w = [x.astype(BF16) for x in p]
        o = [own_heads(dot(w[s], v[s])).astype(BF16) for s in range(3)]
        dv = [dot_tn(w[s], g2[s]).astype(BF16) for s in range(3)]
        ds = [
            (p[s] * (dw[s] - jnp.sum(dw[s] * p[s], axis=-1, keepdims=True)) * scale).astype(BF16) for s in range(3)
        ]
        dq = [own_heads(dot(ds[s], k[s])).astype(BF16) for s in range(3)]
        dk = [dot_tn(ds[s], q2[s]).astype(BF16) for s in range(3)]
        for s in range(3):
            if s < 2:
                att[afters[s], cols] = o[s]
                dq_out[afters[s], cols] = dq[s]
            else:
                last[0, :, cols] = o[s]
                last[1, :, cols] = dq[s]
            for h in range(2):
                pool[base + h * 3 + s, :, pool_cols] = dk[s][h * 128 : h * 128 + 128]
                pool[base + h * 3 + s + 12, :, pool_cols] = dv[s][h * 128 : h * 128 + 128]
        for i in range(2):
            sheet = dot_tn(src[...], pool[pl.ds(base + 12 * i, 6), :, pool_cols].reshape(768, 256))
            grads[t % 3, i] = sheet.reshape(8, 2, 8, 8, 256)
        for copy in onward(t):
            copy.start()

    def sources_back(i):
        cols = pl.ds(pl.multiple_of(i * 256, 256), 256)
        total = sum(
            dot_nt(pool[j * 6 : j * 6 + 6].reshape(768, 1024), w[cols, j % 2 * 1024 : j % 2 * 1024 + 1024])
            for j, w in enumerate((wk, wk, wv, wv))
        )
        pool[24:30, :, cols] = total.astype(BF16).reshape(6, 128, 256)

    def outer_out():
        for i in range(2):
            for j in range(2):
                cols = slice(i * 512 + j * 256, i * 512 + j * 256 + 256)
                sheet = dot_tn(mixed[...], pool[24:30, :, cols].reshape(768, 256))
                grads[1, j, 0:4] = sheet.reshape(4, 2, 8, 8, 256)

            def stack(g, _, i=i):
                for q in range(8):
                    left, right = (grads[1, j, g // 2, g % 2, q] for j in (0, 1))
                    for upper in range(2):
                        rows = slice(upper * 4, upper * 4 + 4)
                        p = 2 * q + upper
                        grads[2, i, g, p // 8, p % 8] = jnp.concatenate([left[rows], right[rows]], axis=0)
                return 0

            lax.fori_loop(0, 8, stack, 0)
        whole_tile(8).start()

    def mixed_back():
        dmix[...] = dot_nt(pool[24:30].reshape(768, 1024), wo[...]).astype(BF16)

    def query_back(half):
        cols = pl.ds(pl.multiple_of(half * 256, 256), 256)
        vcols = pl.ds(pl.multiple_of(half * 256 + 512, 256), 256)
        spans = [slice(s * 64, s * 64 + 64) for s in range(3)]
        k4 = [head_blocks(cond[span, cols]) for span in spans]
        v4 = [head_blocks(cond[span, vcols]) for span in spans]
        dw = [dot_nt(of_span(dmix, s, cols), v4[s]) for s in range(3)]
        p = [of_span(probs, s, cols) for s in range(3)]
        sums = [by_head(dw[s] * p[s], jnp.sum, 0.0) for s in range(3)]
        ds = [(p[s] * (dw[s] - sums[s]) * 0.125).astype(BF16) for s in range(3)]
        for s in range(3):
            dquery = dot(ds[s], k4[s]).astype(BF16)
            for h in range(2):
                rows, part = pl.ds(h * 384 + s * 128, 128), slice(h * 128, h * 128 + 128)
                mixed[rows, cols] = ds[s][part]
                kv[half, rows, :] = dquery[part]
        grads[0, half] = dot_tn(normed[...], kv[half]).reshape(8, 2, 8, 8, 256)
        half_tile(half).start()

    def cond_back():
        def some(i, _):
            s, half = i // 2, i % 2
            span = pl.ds(pl.multiple_of(s * 64, 64), 64)
            cols = pl.ds(pl.multiple_of(half * 256, 256), 256)
            vcols = pl.ds(pl.multiple_of(half * 256 + 512, 256), 256)

            def both(ref):
                parts = [ref[pl.ds(pl.multiple_of(h * 384 + s * 128, 128), 128), cols] for h in range(2)]
                return jnp.concatenate(parts, axis=0)

            w = both(probs).astype(BF16)
            dcond[span, vcols] = head_diagonal(dot_tn(w, both(dmix))).astype(BF16)
            dcond[span, cols] = head_diagonal(dot_tn(both(mixed), both(query))).astype(BF16)
            return 0

        lax.fori_loop(0, 6, some, 0)

    def tile_at(slot, slots):
        return sum(jnp.where(slot == at_slot, t + 1, 0) for t, at_slot in enumerate(slots)) - 1

    def step(slot, _):
        pl.when(slot < 8)(lambda: decode(slot))
        pl.when((slot >= 8) & (slot < 12))(lambda: sources_back(slot - 8))
        pl.when(slot == 12)(outer_out)
        pl.when(slot == 13)(mixed_back)
        pl.when((slot == 14) | (slot == 15))(lambda: query_back(slot - 14))
        pl.when(slot == 16)(cond_back)
        def take_halves(levels):
            for level in levels:
                i = tile_at(slot, HALF_SLOTS[level])
                pl.when(i >= 0)(lambda i=i, level=level: half_tile(i).take(level))

        take_halves((3, 2, 1))
        for level in (3, 2, 1, 0):
            t = tile_at(slot, WHOLE_SLOTS[level])
            pl.when(t >= 0)(lambda t=t, level=level: whole_tile(t).take(level))
        take_halves((0,))
        pl.when(slot < 8)(lambda: whole_tile(slot).start())
        return 0

    lax.fori_loop(0, STEPS, step, 0)

    def arrive(t, _):
        for copy in onward(t):
            copy.wait()
        return 0

    lax.fori_loop(0, 8, arrive, 0)
    followed_by = jnp.where(me == 0, 0.0, 1.0).astype(BF16)
    att[:64, :] = first[0] * followed_by
    dq_out[:64, :] = first[1] * followed_by


def fused(ids, owners, database, cond, gain, wq, wo, wk, wv, queries, grads):
    vmem, smem = pl.BlockSpec(memory_space=pltpu.VMEM), pl.BlockSpec(memory_space=pltpu.SMEM)
    hbm = pl.BlockSpec(memory_space=pl.ANY)
    shape, dma = jax.ShapeDtypeStruct, pltpu.SemaphoreType.DMA
    half = lambda *dims: pltpu.VMEM(dims, BF16)
    full = lambda *dims: pltpu.VMEM(dims, F32)
    outs = pl.pallas_call(
        main_kernel,
        out_shape=(
            shape((192, 2048), BF16),
            shape((192, 2048), BF16),
            shape((192, 1024), BF16),
            shape((8, 512), F32),
            shape((4, 1024), F32),
            shape((8, 2048), F32),
            shape((8, 2048), F32),
        ),
        in_specs=[smem, smem, hbm, hbm, vmem] + [hbm] * 6,
        out_specs=(vmem,) * 7,
        scratch_shapes=[
            half(32, 128, 1024), half(192, 1024), half(1024, 512), half(512, 1024),
            half(1024, 2048), half(1024, 2048), half(192, 2048), half(192, 2048),
            pltpu.VMEM((8, 8, 128), jnp.int32), pltpu.VMEM((8, 8, 128), jnp.int32),
            half(8, 128, 1024), half(8, 64, 1024), half(8, 64, 1024), half(2, 64, 2048),
            half(768, 1024), half(768, 512), full(768, 512), half(768, 512), half(768, 1024),
            half(2, 768, 256), half(768, 512),
            half(2, 64, 2048), half(2, 64, 2048),
            full(3, 2, 8, 2, 8, 8, 256), full(4, 2, 8, 8, 8, 256),
            half(TILES, 3, 16, 16, 256), half(TILES, 3, 16, 16, 256),
            half(TILES, 3, 4, 16, 256), half(TILES, 3, 4, 16, 256),
            half(TILES, 3, 1, 16, 256), half(TILES, 3, 1, 16, 256),
            full(TILES, 16, 16, 256), full(TILES, 4, 16, 256), full(TILES, 1, 16, 256),
            full(2, 8, 8, 8, 256), half(2, 3, 16, 16, 128), half(2, 3, 16, 16, 128),
            full(2, 3, 4, 8, 256), full(2, 3, 4, 8, 256), full(2, 3, 1, 8, 256), full(2, 3, 1, 8, 256),
            full(2, 16, 8, 256), full(2, 4, 8, 256), full(2, 1, 8, 256),
            dma((8,)), dma((8,)), dma((8,)), dma((2, 8)), dma((2, 8)), dma((2, 8)), dma((2, 8)), dma((2, 8)), dma((2, 8)),
            dma((TILES + 2, 10)), dma((TILES + 2, 10)),
        ],
        compiler_params=pltpu.CompilerParams(
            collective_id=0, has_side_effects=True, vmem_limit_bytes=63 * 1024 * 1024
        ),
    )(ids, owners, database, cond, gain, wq, wo, wk, wv, queries, grads)

    def leave(*refs):
        n, sem = len(outs), refs[-1]
        copies = [pltpu.make_async_copy(refs[i], refs[n + i], sem.at[i]) for i in range(n)]
        for copy in copies:
            copy.start()
        for copy in copies:
            copy.wait()

    return pl.pallas_call(
        leave,
        out_shape=tuple(shape(o.shape, o.dtype) for o in outs),
        in_specs=[hbm] * len(outs),
        out_specs=(vmem,) * len(outs),
        scratch_shapes=[dma((len(outs),))],
    )(*outs)


def body(
    queries,
    cond,
    database,
    neighbour_ids,
    owner_map,
    norm_gain,
    w_query_enc,
    w_out_enc,
    w_key_dec,
    w_value_dec,
    cotangent,
):
    return fused(
        neighbour_ids.T,
        owner_map.T,
        database,
        cond,
        norm_gain.reshape(1, -1),
        w_query_enc,
        w_out_enc,
        w_key_dec,
        w_value_dec,
        queries,
        cotangent,
    )


def solution(mesh):
    tokens = P(("seq", "enc"), None)
    return jax.shard_map(
        body,
        mesh=mesh,
        in_specs=(tokens, tokens, P("enc", None, None), tokens, tokens, P(), P(), P(), P(), P(), tokens),
        out_specs=(tokens,) * 7,
        check_vma=False,
    )
```
